768 devices in a mesh: dp: 96 (over x, z, y_lo), tensor: 8 (over y_hi, core).
Axes of the slice: x: 4, y: 8 (y_hi: 4, y_lo: 2; y = y_hi * 2 + y_lo), z: 12, core: 2. Of those that a mesh axis runs over, the one named last changes fastest.
Arguments:
- activations: bfloat16 [36864, 8192], P('dp', 'tensor'), may hold values from -6 to 6
- basis: bfloat16 [8192, 256], replicated, may hold values from -0.0625 to 0.0625
- out_grad: bfloat16 [36864, 14592], P('dp', 'tensor'), may hold values from -0.109375 to 0.109375
- first_moment: float32 [8, 1824, 256], P('tensor', 'dp'), may hold values from -6 to 6
- second_moment: float32 [8, 1824, 256], P('tensor', 'dp'), may hold values from 0.02 to 0.5
Outputs:
- new_first_moment: float32 [8, 1824, 256], P('tensor', 'dp')
- new_second_moment: float32 [8, 1824, 256], P('tensor', 'dp')
- full_update: bfloat16 [8, 1824, 8192], P('tensor', 'dp')
The draws below stay inside these ranges and needn't reach their ends.
All inputs are finite; a program needn't handle non-finite values.
Results may differ from the reference program's by a relative error of at most 0.005.
Values may be sent and summed in bfloat16 or wider, within the bound.
A program may use at most 32 MiB of HBM per device.

```python
import math
import jax
import jax.numpy as jnp
from jax import lax

D = 8192
FF = 14592
R = 256
STEP = 100
TOKENS = 36864
FF_T = 1824
N_TENSOR = 8


def raised(result, stream_key, source, target, blocks, factor):
    def block_of(dim):
        return (jnp.arange(result.shape[dim]) // (result.shape[dim] // blocks)).reshape((-1,) + (1,) * (result.ndim - 1 - dim))

    near = jax.random.permutation(stream_key, blocks)[block_of(target)]
    far = (block_of(target) + blocks // 2) % blocks
    return jnp.where((block_of(source) == near) | (block_of(source) == far), factor * result, result)


def shard_levels(key, dims, split, low, top_value):
    def one(axis_at, blocks):
        steps = jax.random.uniform(jax.random.fold_in(jax.random.fold_in(key, 6), axis_at), (blocks,), jnp.float32, low / len(split), top_value / len(split))
        return jnp.repeat(jnp.exp(steps), dims[axis_at] // blocks).reshape((-1,) + (1,) * (len(dims) - axis_at - 1))

    loudness = one(*split[0])
    for cut in split[1:]:
        loudness = loudness * one(*cut)
    return loudness


def centred(stream_key, extent, width, bound, cuts=(), dtype=jnp.bfloat16):
    factor_of = shard_levels(stream_key, extent, cuts, -0.22, 0.18) if cuts else 1.0
    drawn = jax.random.normal(stream_key, extent, jnp.float32) * width * factor_of
    return jnp.minimum(jnp.maximum(drawn, -bound), bound).astype(dtype)


def bell_draw_with(stream_key, dims, scale, limit, pieces, heavy, held_as=jnp.bfloat16):
    drawn = scale * jax.random.normal(stream_key, dims, jnp.float32)
    if pieces:
        drawn = drawn * shard_levels(stream_key, dims, pieces, -0.22, 0.18)
    return jnp.clip(raised(drawn, jax.random.fold_in(stream_key, 3), *heavy), -limit, limit).astype(held_as)


def setup_inputs(seed: int = 0) -> dict:
    key_of = jax.random.split(jax.random.key(seed), 6)
    return {
        "activations": centred(key_of[0], (TOKENS, D), 1.0, 6.0, ((0, 96), (1, 8))),
        "basis": centred(key_of[1], (D, R), D ** -0.5, 0.0625),
        "out_grad": bell_draw_with(key_of[2], (TOKENS, FF), (TOKENS ** -0.5), 0.109375, ((0, 96), (1, 8)), (0, 1, 96, 4.75)),
        "first_moment": centred(key_of[3], (N_TENSOR, FF_T, R), 1.0, 6.0, ((0, 8), (1, 96)), jnp.float32),
        "second_moment": jnp.clip(jnp.exp(math.log(0.5) - 3.218876 * jax.random.uniform(key_of[4], (N_TENSOR, FF_T, R), jnp.float32) ** shard_levels(key_of[4], (N_TENSOR, FF_T, R), ((0, 8), (1, 96)), -0.2, 0.2)), 0.02, 0.5),
    }


def reference(activations, basis, out_grad, first_moment, second_moment):
    coded_rows = jnp.dot(activations, basis, preferred_element_type=jnp.float32).astype(jnp.bfloat16)
    coded_grad = lax.dot_general(out_grad, coded_rows, (((0,), (0,)), ((), ())), preferred_element_type=jnp.float32)
    coded_grad = coded_grad.reshape(N_TENSOR, FF // N_TENSOR, R)
    new_first = 0.9 * first_moment + 0.1 * coded_grad
    new_second = 0.999 * second_moment + 0.001 * coded_grad * coded_grad
    first_hat = new_first / (1.0 - 0.9 ** STEP)
    second_hat = new_second / (1.0 - 0.999 ** STEP)
    direction = (first_hat / (jnp.sqrt(second_hat) + 1e-08)).astype(jnp.bfloat16)
    update = lax.dot_general(direction.reshape(FF, R), basis, (((1,), (1,)), ((), ())), preferred_element_type=jnp.float32)
    full_update = update.astype(jnp.bfloat16).reshape(N_TENSOR, FF // N_TENSOR, D)
    return (new_first, new_second, full_update)
```

```python
import functools

import jax
import jax.numpy as jnp
from jax import lax
from jax.experimental import pallas as pl
from jax.experimental.pallas import tpu as pltpu
from jax.sharding import PartitionSpec as P

STEP = 100
MESH = pl.DeviceIdType.MESH
F32 = jnp.float32
BF16 = jnp.bfloat16

NX, NZ, NY = 4, 12, 2
NYH, NC = 4, 2
OWN = 19
PAD = 20
PAIRS = NZ // 2
TOK = 48

TENSOR_PEERS = ((2, 0), (2, 1), (1, 0), (3, 0), (1, 1), (3, 1), (0, 1))
XY_PEERS = ((2, 1), (2, 0), (1, 1), (3, 1), (1, 0), (3, 0), (0, 1))
PAIR_STEPS = (3, 2, 4, 1, 5, 0)


def kernel(
    act_hbm, basis_hbm, og_hbm, m_hbm, v_hbm,
    m_out, v_out, upd_out,
    act, rows, basis, og, m_in, v_in,
    part, part_in, code, ogp, chunk, chunk_in, acc, cut, zsend, zin, m_s, v_s,
    load_sem, a_send, a_recv, g_send, g_recv, x_send, x_recv, z_send, z_recv,
):
    dp, t = lax.axis_index("dp"), lax.axis_index("tensor")
    x, z, y = dp // (NZ * NY), lax.rem(dp // NY, NZ), lax.rem(dp, NY)
    yh, core = t // NC, lax.rem(t, NC)
    half = z // 2
    odd = lax.rem(z, 2)

    def tensor_at(k):
        a, c = TENSOR_PEERS[k]
        return lax.rem(yh + a, NYH) * NC + lax.rem(core + c, NC)

    def xy_at(k):
        dx, dy = XY_PEERS[k]
        return lax.rem(x + dx, NX), lax.rem(y + dy, NY)

    feats = act.shape[1]
    start = pl.multiple_of(t * feats, feats)
    loads = [
        pltpu.make_async_copy(act_hbm, act, load_sem.at[0]),
        pltpu.make_async_copy(basis_hbm.at[pl.ds(start, feats)], rows, load_sem.at[1]),
        pltpu.make_async_copy(og_hbm, og, load_sem.at[2]),
        pltpu.make_async_copy(m_hbm, m_in, load_sem.at[3]),
        pltpu.make_async_copy(v_hbm, v_in, load_sem.at[4]),
        pltpu.make_async_copy(basis_hbm, basis, load_sem.at[5]),
    ]
    for load in loads:
        load.start()

    barrier = pltpu.get_barrier_semaphore()
    n_peers = 0
    for dz in range(1, NZ):
        peer = (x * NZ + lax.rem(z + dz, NZ)) * NY + y
        pl.semaphore_signal(barrier, inc=1, device_id=(peer, t), device_id_type=MESH)
        n_peers += 1
    for k in range(len(TENSOR_PEERS)):
        pl.semaphore_signal(barrier, inc=1, device_id=(dp, tensor_at(k)), device_id_type=MESH)
        n_peers += 1
    for k in range(len(XY_PEERS)):
        px, py = xy_at(k)
        peer = (px * NZ + z) * NY + py
        pl.semaphore_signal(barrier, inc=1, device_id=(peer, t), device_id_type=MESH)
        n_peers += 1

    loads[0].wait()
    loads[1].wait()
    coded = jnp.dot(act[...], rows[...], preferred_element_type=F32)
    part[...] = coded.astype(BF16).reshape(part.shape)
    pl.semaphore_wait(barrier, n_peers)

    a_copies = []
    for k in range(len(TENSOR_PEERS)):
        peer = tensor_at(k)
        copy = pltpu.make_async_remote_copy(
            src_ref=part.at[peer], dst_ref=part_in.at[k], send_sem=a_send.at[k], recv_sem=a_recv.at[k],
            device_id=(dp, peer), device_id_type=MESH,
        )
        copy.start()
        a_copies.append(copy)

    loads[2].wait()
    n_out, n_in = 16 * PAD, 16 * OWN
    r = lax.broadcasted_iota(jnp.int32, (n_out, n_in), 0)
    c = lax.broadcasted_iota(jnp.int32, (n_out, n_in), 1)
    quad, in_quad = r // (4 * PAD), lax.rem(r, 4 * PAD)
    place, line = in_quad // PAD, lax.rem(in_quad, PAD)
    owner = quad * 4 + lax.rem(place, 2) * 2 + place // 2
    pick = jnp.where((line < OWN) & (c == owner * OWN + line), 1.0, 0.0).astype(BF16)
    for b in range(NX * NZ * NY // 16):
        moved = jnp.dot(pick, og[b * n_in : (b + 1) * n_in, :], preferred_element_type=F32).astype(BF16)
        for i in range(4):
            ox, oq = (4 * b + i) // PAIRS, (4 * b + i) % PAIRS
            ogp[oq, ox * 4 * PAD : (ox + 1) * 4 * PAD, :] = moved[i * 4 * PAD : (i + 1) * 4 * PAD, :]

    loads[3].wait()
    loads[4].wait()
    m_s[...] = jnp.zeros_like(m_s)
    v_s[...] = jnp.ones_like(v_s)
    for i in range(OWN):
        m_s[i : i + 1, :] = m_in[i]
        v_s[i : i + 1, :] = v_in[i]
    cut[...] = jnp.zeros_like(cut)

    total = part[t].astype(F32)
    for k in range(len(TENSOR_PEERS)):
        a_copies[k].wait_recv()
        total = total + part_in[k].astype(F32)
    code[t] = total.astype(BF16)
    g_copies = []
    for k in range(len(TENSOR_PEERS)):
        peer = tensor_at(k)
        copy = pltpu.make_async_remote_copy(
            src_ref=code.at[t], dst_ref=code.at[t], send_sem=g_send.at[k], recv_sem=g_recv.at[k],
            device_id=(dp, peer), device_id_type=MESH,
        )
        copy.start()
        g_copies.append(copy)
    for copy in g_copies:
        copy.wait_recv()

    coded = code[...].reshape(len(TENSOR_PEERS) * TOK + TOK, code.shape[2])
    x_copies = []
    for j, ahead in enumerate(PAIR_STEPS):
        q = lax.rem(half + ahead, PAIRS)
        term = jnp.dot(ogp[q], coded, preferred_element_type=F32)
        for s in range(NX * NY):
            piece = term[s * 2 * PAD : (s + 1) * 2 * PAD, :]
            chunk[j, s] = jnp.concatenate([piece[:, :128], piece[:, 128:]], axis=0).astype(BF16)
        for k in range(len(XY_PEERS)):
            px, py = xy_at(k)
            copy = pltpu.make_async_remote_copy(
                src_ref=chunk.at[j, px * NY + py], dst_ref=chunk_in.at[j, k],
                send_sem=x_send.at[j, k], recv_sem=x_recv.at[j, k],
                device_id=((px * NZ + z) * NY + py, t), device_id_type=MESH,
            )
            copy.start()
            x_copies.append(copy)

    z_copies = []
    for j, ahead in enumerate(PAIR_STEPS):
        q = lax.rem(half + ahead, PAIRS)
        total = chunk[j, x * NY + y].astype(F32)
        for k in range(len(XY_PEERS)):
            x_copies[j * len(XY_PEERS) + k].wait_recv()
            total = total + chunk_in[j, k].astype(F32)
        acc[...] = total
        for zz in range(2):
            cut[zz, 0:PAD, :] = acc[zz * PAD : (zz + 1) * PAD, :]
            cut[zz, 24 : 24 + PAD, :] = acc[(2 + zz) * PAD : (3 + zz) * PAD, :]
            zsend[j, zz] = cut[zz].astype(BF16)
        which = (0, 1) if ahead else (1 - odd,)
        for zz in which:
            peer = (x * NZ + 2 * q + zz) * NY + y
            at = 2 * j + odd if ahead else 2 * j
            copy = pltpu.make_async_remote_copy(
                src_ref=zsend.at[j, zz], dst_ref=zin.at[at],
                send_sem=z_send.at[len(z_copies)], recv_sem=z_recv.at[at],
                device_id=(peer, t), device_id_type=MESH,
            )
            copy.start()
            z_copies.append(copy)

    total = zsend[PAIRS - 1, odd].astype(F32)
    for i in range(NZ - 1):
        pltpu.make_async_copy(zin.at[i], zin.at[i], z_recv.at[i]).wait()
        total = total + zin[i].astype(F32)
    grad = jnp.concatenate([total[0:24], total[24:48]], axis=1)

    new_first = 0.9 * m_s[...] + 0.1 * grad
    new_second = 0.999 * v_s[...] + 0.001 * grad * grad
    first_hat = new_first / (1.0 - 0.9**STEP)
    second_hat = new_second / (1.0 - 0.999**STEP)
    direction = first_hat / (jnp.sqrt(second_hat) + 1e-08)
    direction = jnp.concatenate([direction, jnp.zeros((8, direction.shape[1]), F32)], axis=0).astype(BF16)
    for i in range(OWN):
        m_out[i] = new_first[i : i + 1, :]
        v_out[i] = new_second[i : i + 1, :]
    loads[5].wait()
    wide = 1024
    for i in range(basis.shape[0] // wide):
        upd = lax.dot_general(
            direction, basis[i * wide : (i + 1) * wide, :], (((1,), (1,)), ((), ())), preferred_element_type=F32
        )
        upd_out[:, i * wide : (i + 1) * wide] = upd[:OWN].astype(BF16)
    for copy in a_copies + g_copies + x_copies + z_copies:
        copy.wait_send()


def on_device(activations, basis, out_grad, first_moment, second_moment):
    d, rank = basis.shape
    tokens, feats = activations.shape
    units = out_grad.shape[1]
    any_spec = pl.BlockSpec(memory_space=pl.ANY)
    vmem_spec = pl.BlockSpec(memory_space=pltpu.VMEM)
    dma = pltpu.SemaphoreType.DMA
    n_ten, n_xy = len(TENSOR_PEERS), len(XY_PEERS)
    new_first, new_second, update = pl.pallas_call(
        kernel,
        out_shape=(
            jax.ShapeDtypeStruct((OWN, 1, rank), F32),
            jax.ShapeDtypeStruct((OWN, 1, rank), F32),
            jax.ShapeDtypeStruct((OWN, d), BF16),
        ),
        in_specs=[any_spec] * 5,
        out_specs=(vmem_spec, vmem_spec, vmem_spec),
        scratch_shapes=[
            pltpu.VMEM((tokens, feats), BF16),
            pltpu.VMEM((feats, rank), BF16),
            pltpu.VMEM((d, rank), BF16),
            pltpu.VMEM((units, tokens), BF16),
            pltpu.VMEM((OWN, 1, rank), F32),
            pltpu.VMEM((OWN, 1, rank), F32),
            pltpu.VMEM((n_ten + 1, TOK, rank), BF16),
            pltpu.VMEM((n_ten, TOK, rank), BF16),
            pltpu.VMEM((n_ten + 1, TOK, rank), BF16),
            pltpu.VMEM((PAIRS, NX * NY * 2 * PAD, tokens), BF16),
            pltpu.VMEM((PAIRS, NX * NY, 4 * PAD, 128), BF16),
            pltpu.VMEM((PAIRS, n_xy, 4 * PAD, 128), BF16),
            pltpu.VMEM((4 * PAD, 128), F32),
            pltpu.VMEM((2, 48, 128), F32),
            pltpu.VMEM((PAIRS, 2, 48, 128), BF16),
            pltpu.VMEM((NZ - 1, 48, 128), BF16),
            pltpu.VMEM((24, rank), F32),
            pltpu.VMEM((24, rank), F32),
            dma((6,)),
            dma((n_ten,)),
            dma((n_ten,)),
            dma((n_ten,)),
            dma((n_ten,)),
            dma((PAIRS, n_xy)),
            dma((PAIRS, n_xy)),
            dma((NZ - 1,)),
            dma((NZ - 1,)),
        ],
        compiler_params=pltpu.CompilerParams(
            collective_id=0, has_side_effects=True, vmem_limit_bytes=60 << 20
        ),
        name="galore_step",
    )(
        activations,
        basis,
        out_grad.T,
        first_moment.transpose(1, 0, 2),
        second_moment.transpose(1, 0, 2),
    )
    return new_first.transpose(1, 0, 2), new_second.transpose(1, 0, 2), update[None]


def solution(mesh):
    placed = (
        P("dp", "tensor"),
        P(),
        P("dp", "tensor"),
        P("tensor", "dp", None),
        P("tensor", "dp", None),
    )
    return jax.shard_map(
        on_device,
        mesh=mesh,
        in_specs=placed,
        out_specs=(P("tensor", "dp", None), P("tensor", "dp", None), P("tensor", "dp", None)),
        check_vma=False,
    )
```

```python
import functools

import jax
import jax.numpy as jnp
from jax import lax
from jax.experimental import pallas as pl
from jax.experimental.pallas import tpu as pltpu
from jax.sharding import PartitionSpec as P

STEP = 100
MESH = pl.DeviceIdType.MESH
F32 = jnp.float32
BF16 = jnp.bfloat16

NX, NZ, NY = 4, 12, 2
NYH, NC = 4, 2
OWN = 19
PAD = 20
QUADS = NZ // 4
TOK = 48
HALF = 128

TENSOR_PEERS = ((2, 0), (2, 1), (1, 0), (3, 0), (1, 1), (3, 1), (0, 1))
XY_PEERS = ((2, 0), (1, 1), (3, 1), (1, 0), (3, 0), (0, 1))
FAR_PEER = (2, 1)
QUAD_STEPS = (1, 2, 0)


def reduce_kernel(
    act_hbm, basis_hbm, og_hbm, m_hbm, v_hbm,
    grad_out, turned_out, m_out, v_out,
    act, rows, basis, og, m_in, v_in,
    part, part_in, code, ogp, chunk, chunk_in, acc, far_acc, far_send, far_in, far_sum, far_got, near_acc, near_send, near_in,
    load_sem, a_send, a_recv, g_send, g_recv, x_send, x_recv, f_send, f_recv, l_send, l_recv, z_send, z_recv,
):
    dp, t = lax.axis_index("dp"), lax.axis_index("tensor")
    x, z, y = dp // (NZ * NY), lax.rem(dp // NY, NZ), lax.rem(dp, NY)
    yh, core = t // NC, lax.rem(t, NC)
    own_quad, own_place = z // 4, lax.rem(z, 4)
    n_ten, n_xy = len(TENSOR_PEERS), len(XY_PEERS)

    def tensor_at(k):
        a, c = TENSOR_PEERS[k]
        return lax.rem(yh + a, NYH) * NC + lax.rem(core + c, NC)

    def xy_at(k):
        dx, dy = XY_PEERS[k]
        return lax.rem(x + dx, NX), lax.rem(y + dy, NY)

    def dp_at(px, pz, py):
        return (lax.rem(px, NX) * NZ + lax.rem(pz, NZ)) * NY + lax.rem(py, NY)

    barrier = pltpu.get_barrier_semaphore()

    def signal(to_dp, to_t):
        pl.semaphore_signal(barrier, inc=1, device_id=(to_dp, to_t), device_id_type=MESH)

    for dz in (6, 5, 7, 4, 8, 3, 9, 2, 10, 1, 11):
        signal(dp_at(x, z + dz, y), t)
    for k in range(n_ten):
        signal(dp, tensor_at(k))
    far_dp = dp_at(x + FAR_PEER[0], z, y + FAR_PEER[1])
    signal(far_dp, t)
    for dx, dy in XY_PEERS:
        signal(dp_at(x + dx, z, y + dy), t)

    tokens, feats = act.shape
    start = pl.multiple_of(t * feats, feats)
    n_cut = 4
    first_loads = []
    for i in range(n_cut):
        n = feats // n_cut
        first_loads.append(
            pltpu.make_async_copy(
                basis_hbm.at[pl.ds(start + i * n, n)], rows.at[pl.ds(i * n, n)], load_sem.at[i]
            )
        )
        n = tokens // n_cut
        first_loads.append(
            pltpu.make_async_copy(
                act_hbm.at[pl.ds(i * n, n)], act.at[pl.ds(i * n, n)], load_sem.at[n_cut + i]
            )
        )
    og_load = pltpu.make_async_copy(og_hbm, og, load_sem.at[2 * n_cut])
    m_load = pltpu.make_async_copy(m_hbm, m_in, load_sem.at[2 * n_cut + 1])
    v_load = pltpu.make_async_copy(v_hbm, v_in, load_sem.at[2 * n_cut + 2])
    basis_load = pltpu.make_async_copy(basis_hbm, basis, load_sem.at[2 * n_cut + 3])
    for load in first_loads:
        load.start()

    for load in first_loads:
        load.wait()
    og_load.start()
    m_load.start()
    v_load.start()
    basis_load.start()
    a_copies = []
    for h in range(2):
        coded = jnp.dot(act[...], rows[:, h * HALF : (h + 1) * HALF], preferred_element_type=F32)
        part[h] = coded.astype(BF16).reshape(part.shape[1:])
        if h == 0:
            pl.semaphore_wait(barrier, NZ - 1 + n_ten + 1 + n_xy)
        for k in range(n_ten):
            peer = tensor_at(k)
            copy = pltpu.make_async_remote_copy(
                src_ref=part.at[h, peer], dst_ref=part_in.at[h, k],
                send_sem=a_send.at[h, k], recv_sem=a_recv.at[h, k],
                device_id=(dp, peer), device_id_type=MESH,
            )
            copy.start()
            a_copies.append(copy)

    og_load.wait()
    n_out, n_in = 16 * PAD, 16 * OWN
    unit_rows = 8 * PAD
    r = lax.broadcasted_iota(jnp.int32, (n_out, n_in), 0)
    c = lax.broadcasted_iota(jnp.int32, (n_out, n_in), 1)
    unit, in_unit = r // unit_rows, lax.rem(r, unit_rows)
    place, line = in_unit // PAD, lax.rem(in_unit, PAD)
    owner = unit * 8 + lax.rem(place, 4) * 2 + place // 4
    pick = jnp.where((line < OWN) & (c == owner * OWN + line), 1.0, 0.0).astype(BF16)
    for b in range(NX * NZ * NY // 16):
        moved = jnp.dot(pick, og[b * n_in : (b + 1) * n_in, :], preferred_element_type=F32).astype(BF16)
        for i in range(2):
            ox, oq = (2 * b + i) // QUADS, (2 * b + i) % QUADS
            ogp[oq, ox * unit_rows : (ox + 1) * unit_rows, :] = moved[i * unit_rows : (i + 1) * unit_rows, :]
    far_acc[...] = jnp.zeros_like(far_acc)
    near_acc[...] = jnp.zeros_like(near_acc)

    g_copies = []
    for h in range(2):
        total = part[h, t].astype(F32)
        for k in range(n_ten):
            a_copies[h * n_ten + k].wait_recv()
            total = total + part_in[h, k].astype(F32)
        code[h, t] = total.astype(BF16)
        for k in range(n_ten):
            copy = pltpu.make_async_remote_copy(
                src_ref=code.at[h, t], dst_ref=code.at[h, t],
                send_sem=g_send.at[h, k], recv_sem=g_recv.at[h, k],
                device_id=(dp, tensor_at(k)), device_id_type=MESH,
            )
            copy.start()
            g_copies.append(copy)

    m_load.wait()
    v_load.wait()
    m_out[...] = jnp.zeros_like(m_out)
    v_out[...] = jnp.ones_like(v_out)
    for i in range(OWN):
        m_out[i : i + 1, :] = m_in[i]
        v_out[i : i + 1, :] = v_in[i]
    basis_load.wait()
    wide = 1024
    for i in range(basis.shape[0] // wide):
        turned_out[:, i * wide : (i + 1) * wide] = basis[i * wide : (i + 1) * wide, :].T

    def along_z(src, dst, send_sem, recv_sem):
        copies = []
        for j, ahead in enumerate(QUAD_STEPS):
            copies.append([])
            for e in range(0 if ahead else 1, 4):
                zz = e if ahead else lax.rem(own_place + e, 4)
                to = 4 * lax.rem(own_quad + ahead, QUADS) + zz
                slot = lax.rem(to - z + NZ, NZ) - 1
                copies[j].append(
                    pltpu.make_async_remote_copy(
                        src_ref=src.at[j, zz], dst_ref=dst.at[slot],
                        send_sem=send_sem.at[4 * j + e - (not ahead)], recv_sem=recv_sem.at[slot],
                        device_id=((x * NZ + to) * NY + y, t), device_id_type=MESH,
                    )
                )
        return copies

    def sum_along_z(src, dst, recv_sem):
        total = src[QUADS - 1, own_place].astype(F32)
        for i in range(NZ - 1):
            pltpu.make_async_copy(dst.at[i], dst.at[i], recv_sem.at[i]).wait()
            total = total + dst[i].astype(F32)
        return total

    far_copies = along_z(far_send, far_in, f_send, f_recv)
    near_copies = along_z(near_send, near_in, z_send, z_recv)
    far_place = lax.rem(x + FAR_PEER[0], NX) * NY + lax.rem(y + FAR_PEER[1], NY)
    far_rows = pl.ds(pl.multiple_of(far_place * 4 * PAD, 4 * PAD), 4 * PAD)
    x_copies = []
    for h in range(2):
        for k in range(n_ten):
            g_copies[h * n_ten + k].wait_recv()
        coded = code[h].reshape((n_ten + 1) * TOK, HALF)

        def far_part():
            for j, ahead in enumerate(QUAD_STEPS):
                q = lax.rem(own_quad + ahead, QUADS)
                acc[...] = jnp.dot(ogp[q, far_rows, :], coded, preferred_element_type=F32)
                for zz in range(4):
                    far_acc[j, zz, 24 * h : 24 * h + PAD, :] = acc[zz * PAD : (zz + 1) * PAD, :]

        if h == 1:
            far_part()
            for j in range(QUADS):
                for zz in range(4):
                    far_send[j, zz] = far_acc[j, zz].astype(BF16)
                for copy in far_copies[j]:
                    copy.start()
        for j, ahead in enumerate(QUAD_STEPS):
            q = lax.rem(own_quad + ahead, QUADS)
            at = h * QUADS + j
            term = jnp.dot(ogp[q], coded, preferred_element_type=F32)
            chunk[at] = term.astype(BF16).reshape(chunk.shape[1:])
            for k in range(n_xy):
                px, py = xy_at(k)
                copy = pltpu.make_async_remote_copy(
                    src_ref=chunk.at[at, px * NY + py], dst_ref=chunk_in.at[at, k],
                    send_sem=x_send.at[at, k], recv_sem=x_recv.at[at, k],
                    device_id=((px * NZ + z) * NY + py, t), device_id_type=MESH,
                )
                copy.start()
                x_copies.append(copy)
        if h == 0:
            far_part()

    far_copy = pltpu.make_async_remote_copy(
        src_ref=far_sum, dst_ref=far_got, send_sem=l_send, recv_sem=l_recv, device_id=(far_dp, t), device_id_type=MESH
    )
    for h in range(2):
        for j in range(QUADS):
            at = h * QUADS + j
            if at == 2 * QUADS - 1:
                far_sum[...] = sum_along_z(far_send, far_in, f_recv).astype(BF16)
                far_copy.start()
            total = chunk[at, x * NY + y].astype(F32)
            for k in range(n_xy):
                x_copies[at * n_xy + k].wait_recv()
                total = total + chunk_in[at, k].astype(F32)
            acc[...] = total
            for zz in range(4):
                near_acc[j, zz, 24 * h : 24 * h + PAD, :] = acc[zz * PAD : (zz + 1) * PAD, :]
            if h == 1:
                for zz in range(4):
                    near_send[j, zz] = near_acc[j, zz].astype(BF16)
                for copy in near_copies[j]:
                    copy.start()

    total = sum_along_z(near_send, near_in, z_recv)
    far_copy.wait_recv()
    total = total + far_got[...].astype(F32)
    grad_out[...] = jnp.concatenate([total[0:24], total[24:48]], axis=1)
    z_copies = [far_copy] + sum(far_copies + near_copies, [])
    for copy in a_copies + g_copies + x_copies + z_copies:
        copy.wait_send()


def step_kernel(grad, turned, m, v, m_hbm, v_hbm, upd_hbm, m_rows, v_rows, upd, sem):
    g = grad[...]
    new_first = 0.9 * m[...] + 0.1 * g
    new_second = 0.999 * v[...] + 0.001 * g * g
    first_hat = new_first / (1.0 - 0.9**STEP)
    second_hat = new_second / (1.0 - 0.999**STEP)
    direction = first_hat / (jnp.sqrt(second_hat) + 1e-08)
    direction = jnp.concatenate([direction, jnp.zeros((8, direction.shape[1]), F32)], axis=0).astype(BF16)
    wide = 2048
    saves = []
    for i in range(turned.shape[1] // wide):
        cols = pl.ds(i * wide, wide)
        upd[:, cols] = jnp.dot(direction, turned[:, cols], preferred_element_type=F32)[:OWN].astype(BF16)
        save = pltpu.make_async_copy(upd.at[:, cols], upd_hbm.at[:, cols], sem.at[i])
        save.start()
        saves.append(save)
    for i in range(OWN):
        m_rows[i] = new_first[i : i + 1, :]
        v_rows[i] = new_second[i : i + 1, :]
    saves.append(pltpu.make_async_copy(m_rows, m_hbm, sem.at[4]))
    saves.append(pltpu.make_async_copy(v_rows, v_hbm, sem.at[5]))
    saves[-2].start()
    saves[-1].start()
    for save in saves:
        save.wait()


def on_device(activations, basis, out_grad, first_moment, second_moment):
    d, rank = basis.shape
    tokens, feats = activations.shape
    units = out_grad.shape[1]
    hbm = pl.BlockSpec(memory_space=pltpu.HBM)
    vmem = pl.BlockSpec(memory_space=pltpu.VMEM)
    dma = pltpu.SemaphoreType.DMA
    n_ten, n_xy = len(TENSOR_PEERS), len(XY_PEERS)
    steps = 2 * QUADS
    grad, turned, m, v = pl.pallas_call(
        reduce_kernel,
        out_shape=(
            jax.ShapeDtypeStruct((24, rank), F32),
            jax.ShapeDtypeStruct((rank, d), BF16),
            jax.ShapeDtypeStruct((24, rank), F32),
            jax.ShapeDtypeStruct((24, rank), F32),
        ),
        in_specs=[hbm] * 5,
        out_specs=(vmem,) * 4,
        scratch_shapes=[
            pltpu.VMEM((tokens, feats), BF16),
            pltpu.VMEM((feats, rank), BF16),
            pltpu.VMEM((d, rank), BF16),
            pltpu.VMEM((units, tokens), BF16),
            pltpu.VMEM((OWN, 1, rank), F32),
            pltpu.VMEM((OWN, 1, rank), F32),
            pltpu.VMEM((2, n_ten + 1, TOK, HALF), BF16),
            pltpu.VMEM((2, n_ten, TOK, HALF), BF16),
            pltpu.VMEM((2, n_ten + 1, TOK, HALF), BF16),
            pltpu.VMEM((QUADS, NX * NY * 4 * PAD, tokens), BF16),
            pltpu.VMEM((steps, NX * NY, 4 * PAD, HALF), BF16),
            pltpu.VMEM((steps, n_xy, 4 * PAD, HALF), BF16),
            pltpu.VMEM((4 * PAD, HALF), F32),
            pltpu.VMEM((QUADS, 4, 48, HALF), F32),
            pltpu.VMEM((QUADS, 4, 48, HALF), BF16),
            pltpu.VMEM((NZ - 1, 48, HALF), BF16),
            pltpu.VMEM((48, HALF), BF16),
            pltpu.VMEM((48, HALF), BF16),
            pltpu.VMEM((QUADS, 4, 48, HALF), F32),
            pltpu.VMEM((QUADS, 4, 48, HALF), BF16),
            pltpu.VMEM((NZ - 1, 48, HALF), BF16),
            dma((12,)),
            dma((2, n_ten)),
            dma((2, n_ten)),
            dma((2, n_ten)),
            dma((2, n_ten)),
            dma((steps, n_xy)),
            dma((steps, n_xy)),
            dma((NZ - 1,)),
            dma((NZ - 1,)),
            dma,
            dma,
            dma((NZ - 1,)),
            dma((NZ - 1,)),
        ],
        compiler_params=pltpu.CompilerParams(
            collective_id=0, has_side_effects=True, vmem_limit_bytes=40 << 20
        ),
        name="reduce_gradient",
    )(*[
        pltpu.with_memory_space_constraint(a, pltpu.HBM)
        for a in (
            activations,
            basis,
            out_grad.T,
            first_moment.transpose(1, 0, 2),
            second_moment.transpose(1, 0, 2),
        )
    ])
    new_first, new_second, update = pl.pallas_call(
        step_kernel,
        out_shape=(
            jax.ShapeDtypeStruct((OWN, 1, rank), F32),
            jax.ShapeDtypeStruct((OWN, 1, rank), F32),
            jax.ShapeDtypeStruct((OWN, d), BF16),
        ),
        in_specs=[vmem] * 4,
        out_specs=(hbm,) * 3,
        scratch_shapes=[
            pltpu.VMEM((OWN, 1, rank), F32),
            pltpu.VMEM((OWN, 1, rank), F32),
            pltpu.VMEM((OWN, d), BF16),
            dma((6,)),
        ],
        compiler_params=pltpu.CompilerParams(vmem_limit_bytes=16 << 20),
        name="adam_update",
    )(grad, turned, m, v)
    return new_first.transpose(1, 0, 2), new_second.transpose(1, 0, 2), update[None]


def solution(mesh):
    placed = (
        P("dp", "tensor"),
        P(),
        P("dp", "tensor"),
        P("tensor", "dp", None),
        P("tensor", "dp", None),
    )
    return jax.shard_map(
        on_device,
        mesh=mesh,
        in_specs=placed,
        out_specs=(P("tensor", "dp", None), P("tensor", "dp", None), P("tensor", "dp", None)),
        check_vma=False,
    )
```

```python
import functools

import jax
import jax.numpy as jnp
from jax import lax
from jax.experimental import pallas as pl
from jax.experimental.pallas import tpu as pltpu
from jax.sharding import PartitionSpec as P

STEP = 100
MESH = pl.DeviceIdType.MESH
F32 = jnp.float32
BF16 = jnp.bfloat16

NX, NZ, NY = 4, 12, 2
NYH, NC = 4, 2
OWN = 19
PAD = 20
QUADS = NZ // 4
TOK = 48
HALF = 128

TENSOR_PEERS = ((2, 0), (2, 1), (1, 0), (3, 0), (1, 1), (3, 1), (0, 1))
XY_PEERS = ((2, 0), (1, 1), (3, 1), (1, 0), (3, 0), (0, 1))
FAR_PEER = (2, 1)
MERGED_ROUTES = (((1, 0), (1, 1)), ((3, 0), (3, 1)), ((2, 0), (2, 0)), ((1, 0), (1, 0)), ((3, 0), (3, 0)))
DIRECT_ROUTES = tuple((p, p) for p in XY_PEERS)
QUAD_STEPS = (1, 2, 0)


def reduce_kernel(
    act_hbm, basis_hbm, og_hbm, m_hbm, v_hbm,
    grad_out, turned_out, m_out, v_out,
    act, rows, basis, og, m_in, v_in,
    part, part_in, code, ogp, chunk, chunk_in, merged, acc, far_acc, far_send, far_in, far_sum, far_got, near_acc, near_send, near_in,
    load_sem, a_send, a_recv, g_send, g_recv, x_send, x_recv, f_send, f_recv, l_send, l_recv, z_send, z_recv, hello,
):
    dp, t = lax.axis_index("dp"), lax.axis_index("tensor")
    x, z, y = dp // (NZ * NY), lax.rem(dp // NY, NZ), lax.rem(dp, NY)
    yh, core = t // NC, lax.rem(t, NC)
    own_quad, own_place = z // 4, lax.rem(z, 4)
    n_ten, n_xy = len(TENSOR_PEERS), len(XY_PEERS)

    def tensor_at(k):
        a, c = TENSOR_PEERS[k]
        return lax.rem(yh + a, NYH) * NC + lax.rem(core + c, NC)

    def xy_at(place):
        dx, dy = place
        return lax.rem(x + dx, NX), lax.rem(y + dy, NY)

    def dp_at(px, pz, py):
        return (lax.rem(px, NX) * NZ + lax.rem(pz, NZ)) * NY + lax.rem(py, NY)

    barrier = pltpu.get_barrier_semaphore()

    def signal(to_dp, to_t):
        pl.semaphore_signal(barrier, inc=1, device_id=(to_dp, to_t), device_id_type=MESH)

    for k in range(n_ten):
        signal(dp, tensor_at(k))
    for dz in (3, 9, 2, 10, 1, 11):
        signal(dp_at(x, z + dz, y), t)
    far_dp = dp_at(x + FAR_PEER[0], z, y + FAR_PEER[1])
    signal(far_dp, t)
    for dx, dy in XY_PEERS:
        signal(dp_at(x + dx, z, y + dy), t)

    tokens, feats = act.shape
    start = pl.multiple_of(t * feats, feats)
    n_cut = 4
    first_loads = []
    for i in range(n_cut):
        n = feats // n_cut
        first_loads.append(
            pltpu.make_async_copy(
                basis_hbm.at[pl.ds(start + i * n, n)], rows.at[pl.ds(i * n, n)], load_sem.at[i]
            )
        )
        n = tokens // n_cut
        first_loads.append(
            pltpu.make_async_copy(
                act_hbm.at[pl.ds(i * n, n)], act.at[pl.ds(i * n, n)], load_sem.at[n_cut + i]
            )
        )
    og_load = pltpu.make_async_copy(og_hbm, og, load_sem.at[2 * n_cut])
    m_load = pltpu.make_async_copy(m_hbm, m_in, load_sem.at[2 * n_cut + 1])
    v_load = pltpu.make_async_copy(v_hbm, v_in, load_sem.at[2 * n_cut + 2])
    basis_load = pltpu.make_async_copy(basis_hbm, basis, load_sem.at[2 * n_cut + 3])
    for load in first_loads:
        load.start()

    for load in first_loads:
        load.wait()
    og_load.start()
    m_load.start()
    v_load.start()
    basis_load.start()
    a_copies = []
    for h in range(2):
        coded = jnp.dot(act[...], rows[:, h * HALF : (h + 1) * HALF], preferred_element_type=F32)
        part[h] = coded.astype(BF16).reshape(part.shape[1:])
        if h == 0:
            pl.semaphore_wait(barrier, n_ten + 6 + 1 + n_xy)
            for i, dz in enumerate((3, NZ - 3)):
                pl.semaphore_signal(
                    hello.at[i], inc=1, device_id=(dp_at(x, z + dz, y), t), device_id_type=MESH
                )
        for k in range(n_ten):
            peer = tensor_at(k)
            copy = pltpu.make_async_remote_copy(
                src_ref=part.at[h, peer], dst_ref=part_in.at[h, k],
                send_sem=a_send.at[h, k], recv_sem=a_recv.at[h, k],
                device_id=(dp, peer), device_id_type=MESH,
            )
            copy.start()
            a_copies.append(copy)

    og_load.wait()
    n_out, n_in = 16 * PAD, 16 * OWN
    unit_rows = 8 * PAD
    r = lax.broadcasted_iota(jnp.int32, (n_out, n_in), 0)
    c = lax.broadcasted_iota(jnp.int32, (n_out, n_in), 1)
    unit, in_unit = r // unit_rows, lax.rem(r, unit_rows)
    place, line = in_unit // PAD, lax.rem(in_unit, PAD)
    owner = unit * 8 + lax.rem(place, 4) * 2 + place // 4
    pick = jnp.where((line < OWN) & (c == owner * OWN + line), 1.0, 0.0).astype(BF16)
    for b in range(NX * NZ * NY // 16):
        moved = jnp.dot(pick, og[b * n_in : (b + 1) * n_in, :], preferred_element_type=F32).astype(BF16)
        for i in range(2):
            ox, oq = (2 * b + i) // QUADS, (2 * b + i) % QUADS
            ogp[oq, ox * unit_rows : (ox + 1) * unit_rows, :] = moved[i * unit_rows : (i + 1) * unit_rows, :]
    far_acc[...] = jnp.zeros_like(far_acc)
    near_acc[...] = jnp.zeros_like(near_acc)

    g_copies = []
    for h in range(2):
        total = part[h, t].astype(F32)
        for k in range(n_ten):
            a_copies[h * n_ten + k].wait_recv()
            total = total + part_in[h, k].astype(F32)
        code[h, t] = total.astype(BF16)
        for k in range(n_ten):
            copy = pltpu.make_async_remote_copy(
                src_ref=code.at[h, t], dst_ref=code.at[h, t],
                send_sem=g_send.at[h, k], recv_sem=g_recv.at[h, k],
                device_id=(dp, tensor_at(k)), device_id_type=MESH,
            )
            copy.start()
            g_copies.append(copy)

    m_load.wait()
    v_load.wait()
    m_out[...] = jnp.zeros_like(m_out)
    v_out[...] = jnp.ones_like(v_out)
    for i in range(OWN):
        m_out[i : i + 1, :] = m_in[i]
        v_out[i : i + 1, :] = v_in[i]
    basis_load.wait()
    wide = 1024
    for i in range(basis.shape[0] // wide):
        turned_out[:, i * wide : (i + 1) * wide] = basis[i * wide : (i + 1) * wide, :].T

    def along_z(src, dst, send_sem, recv_sem):
        copies = []
        for j, ahead in enumerate(QUAD_STEPS):
            copies.append([])
            for e in range(0 if ahead else 1, 4):
                zz = e if ahead else lax.rem(own_place + e, 4)
                to = 4 * lax.rem(own_quad + ahead, QUADS) + zz
                slot = lax.rem(to - z + NZ, NZ) - 1
                copies[j].append(
                    pltpu.make_async_remote_copy(
                        src_ref=src.at[j, zz], dst_ref=dst.at[slot],
                        send_sem=send_sem.at[4 * j + e - (not ahead)], recv_sem=recv_sem.at[slot],
                        device_id=((x * NZ + to) * NY + y, t), device_id_type=MESH,
                    )
                )
        return copies

    def sum_along_z(src, dst, recv_sem):
        total = src[QUADS - 1, own_place].astype(F32)
        for i in range(NZ - 1):
            pltpu.make_async_copy(dst.at[i], dst.at[i], recv_sem.at[i]).wait()
            total = total + dst[i].astype(F32)
        return total

    far_copies = along_z(far_send, far_in, f_send, f_recv)
    near_copies = along_z(near_send, near_in, z_send, z_recv)
    far_place = lax.rem(x + FAR_PEER[0], NX) * NY + lax.rem(y + FAR_PEER[1], NY)
    far_rows = pl.ds(pl.multiple_of(far_place * 4 * PAD, 4 * PAD), 4 * PAD)
    x_copies = [[] for _ in range(2 * QUADS)]
    for h in range(2):
        for k in range(n_ten):
            g_copies[h * n_ten + k].wait_recv()
        coded = code[h].reshape((n_ten + 1) * TOK, HALF)

        def far_part():
            for j, ahead in enumerate(QUAD_STEPS):
                q = lax.rem(own_quad + ahead, QUADS)
                acc[...] = jnp.dot(ogp[q, far_rows, :], coded, preferred_element_type=F32)
                for zz in range(4):
                    far_acc[j, zz, 24 * h : 24 * h + PAD, :] = acc[zz * PAD : (zz + 1) * PAD, :]

        if h == 1:
            far_part()
            for i in range(2):
                pl.semaphore_wait(hello.at[i], 1)
            for j in range(QUADS):
                for zz in range(4):
                    far_send[j, zz] = far_acc[j, zz].astype(BF16)
                for copy in far_copies[j]:
                    copy.start()
        for j, ahead in enumerate(QUAD_STEPS):
            q = lax.rem(own_quad + ahead, QUADS)
            at = h * QUADS + j
            term = jnp.dot(ogp[q], coded, preferred_element_type=F32)
            chunk[at] = term.astype(BF16).reshape(chunk.shape[1:])
            for k, (to, share) in enumerate(DIRECT_ROUTES if h else MERGED_ROUTES):
                px, py = xy_at(to)
                sx, sy = xy_at(share)
                copy = pltpu.make_async_remote_copy(
                    src_ref=chunk.at[at, sx * NY + sy], dst_ref=chunk_in.at[at, k],
                    send_sem=x_send.at[at, k], recv_sem=x_recv.at[at, k],
                    device_id=((px * NZ + z) * NY + py, t), device_id_type=MESH,
                )
                copy.start()
                x_copies[at].append(copy)
        if h == 0:
            far_part()

    far_copy = pltpu.make_async_remote_copy(
        src_ref=far_sum, dst_ref=far_got, send_sem=l_send, recv_sem=l_recv, device_id=(far_dp, t), device_id_type=MESH
    )
    for j in range(QUADS):
        total = chunk[j, x * NY + 1 - y].astype(F32)
        for k in range(2):
            x_copies[j][k].wait_recv()
            total = total + chunk_in[j, k].astype(F32)
        merged[j] = total.astype(BF16)
        copy = pltpu.make_async_remote_copy(
            src_ref=merged.at[j], dst_ref=chunk_in.at[j, 5], send_sem=x_send.at[j, 5], recv_sem=x_recv.at[j, 5],
            device_id=(dp_at(x, z, y + 1), t), device_id_type=MESH,
        )
        copy.start()
        x_copies[j].append(copy)
    for j in range(QUADS):
        if j == QUADS - 1:
            far_sum[...] = sum_along_z(far_send, far_in, f_recv).astype(BF16)
            far_copy.start()
        for h in range(2):
            at = h * QUADS + j
            total = chunk[at, x * NY + y].astype(F32)
            for k in range(0 if h else 2, n_xy):
                x_copies[at][k].wait_recv()
                total = total + chunk_in[at, k].astype(F32)
            acc[...] = total
            for zz in range(4):
                near_acc[j, zz, 24 * h : 24 * h + PAD, :] = acc[zz * PAD : (zz + 1) * PAD, :]
        for zz in range(4):
            near_send[j, zz] = near_acc[j, zz].astype(BF16)
        for copy in near_copies[j]:
            copy.start()

    total = sum_along_z(near_send, near_in, z_recv)
    far_copy.wait_recv()
    total = total + far_got[...].astype(F32)
    grad_out[...] = jnp.concatenate([total[0:24], total[24:48]], axis=1)
    z_copies = [far_copy] + sum(far_copies + near_copies + x_copies, [])
    for copy in a_copies + g_copies + z_copies:
        copy.wait_send()


def step_kernel(grad, turned, m, v, m_hbm, v_hbm, upd_hbm, m_rows, v_rows, upd, sem):
    g = grad[...]
    new_first = 0.9 * m[...] + 0.1 * g
    new_second = 0.999 * v[...] + 0.001 * g * g
    first_hat = new_first / (1.0 - 0.9**STEP)
    second_hat = new_second / (1.0 - 0.999**STEP)
    direction = first_hat / (jnp.sqrt(second_hat) + 1e-08)
    direction = jnp.concatenate([direction, jnp.zeros((8, direction.shape[1]), F32)], axis=0).astype(BF16)
    wide = 2048
    saves = []
    for i in range(turned.shape[1] // wide):
        cols = pl.ds(i * wide, wide)
        upd[:, cols] = jnp.dot(direction, turned[:, cols], preferred_element_type=F32)[:OWN].astype(BF16)
        save = pltpu.make_async_copy(upd.at[:, cols], upd_hbm.at[:, cols], sem.at[i])
        save.start()
        saves.append(save)
    for i in range(OWN):
        m_rows[i] = new_first[i : i + 1, :]
        v_rows[i] = new_second[i : i + 1, :]
    saves.append(pltpu.make_async_copy(m_rows, m_hbm, sem.at[4]))
    saves.append(pltpu.make_async_copy(v_rows, v_hbm, sem.at[5]))
    saves[-2].start()
    saves[-1].start()
    for save in saves:
        save.wait()


def on_device(activations, basis, out_grad, first_moment, second_moment):
    d, rank = basis.shape
    tokens, feats = activations.shape
    units = out_grad.shape[1]
    hbm = pl.BlockSpec(memory_space=pltpu.HBM)
    vmem = pl.BlockSpec(memory_space=pltpu.VMEM)
    dma = pltpu.SemaphoreType.DMA
    n_ten, n_xy = len(TENSOR_PEERS), len(XY_PEERS)
    steps = 2 * QUADS
    grad, turned, m, v = pl.pallas_call(
        reduce_kernel,
        out_shape=(
            jax.ShapeDtypeStruct((24, rank), F32),
            jax.ShapeDtypeStruct((rank, d), BF16),
            jax.ShapeDtypeStruct((24, rank), F32),
            jax.ShapeDtypeStruct((24, rank), F32),
        ),
        in_specs=[hbm] * 5,
        out_specs=(vmem,) * 4,
        scratch_shapes=[
            pltpu.VMEM((tokens, feats), BF16),
            pltpu.VMEM((feats, rank), BF16),
            pltpu.VMEM((d, rank), BF16),
            pltpu.VMEM((units, tokens), BF16),
            pltpu.VMEM((OWN, 1, rank), F32),
            pltpu.VMEM((OWN, 1, rank), F32),
            pltpu.VMEM((2, n_ten + 1, TOK, HALF), BF16),
            pltpu.VMEM((2, n_ten, TOK, HALF), BF16),
            pltpu.VMEM((2, n_ten + 1, TOK, HALF), BF16),
            pltpu.VMEM((QUADS, NX * NY * 4 * PAD, tokens), BF16),
            pltpu.VMEM((steps, NX * NY, 4 * PAD, HALF), BF16),
            pltpu.VMEM((steps, n_xy, 4 * PAD, HALF), BF16),
            pltpu.VMEM((QUADS, 4 * PAD, HALF), BF16),
            pltpu.VMEM((4 * PAD, HALF), F32),
            pltpu.VMEM((QUADS, 4, 48, HALF), F32),
            pltpu.VMEM((QUADS, 4, 48, HALF), BF16),
            pltpu.VMEM((NZ - 1, 48, HALF), BF16),
            pltpu.VMEM((48, HALF), BF16),
            pltpu.VMEM((48, HALF), BF16),
            pltpu.VMEM((QUADS, 4, 48, HALF), F32),
            pltpu.VMEM((QUADS, 4, 48, HALF), BF16),
            pltpu.VMEM((NZ - 1, 48, HALF), BF16),
            dma((12,)),
            dma((2, n_ten)),
            dma((2, n_ten)),
            dma((2, n_ten)),
            dma((2, n_ten)),
            dma((steps, n_xy)),
            dma((steps, n_xy)),
            dma((NZ - 1,)),
            dma((NZ - 1,)),
            dma,
            dma,
            dma((NZ - 1,)),
            dma((NZ - 1,)),
            pltpu.SemaphoreType.REGULAR((2,)),
        ],
        compiler_params=pltpu.CompilerParams(
            collective_id=0, has_side_effects=True, vmem_limit_bytes=40 << 20
        ),
        name="reduce_gradient",
    )(*[
        pltpu.with_memory_space_constraint(a, pltpu.HBM)
        for a in (
            activations,
            basis,
            out_grad.T,
            first_moment.transpose(1, 0, 2),
            second_moment.transpose(1, 0, 2),
        )
    ])
    new_first, new_second, update = pl.pallas_call(
        step_kernel,
        out_shape=(
            jax.ShapeDtypeStruct((OWN, 1, rank), F32),
            jax.ShapeDtypeStruct((OWN, 1, rank), F32),
            jax.ShapeDtypeStruct((OWN, d), BF16),
        ),
        in_specs=[vmem] * 4,
        out_specs=(hbm,) * 3,
        scratch_shapes=[
            pltpu.VMEM((OWN, 1, rank), F32),
            pltpu.VMEM((OWN, 1, rank), F32),
            pltpu.VMEM((OWN, d), BF16),
            dma((6,)),
        ],
        compiler_params=pltpu.CompilerParams(vmem_limit_bytes=16 << 20),
        name="adam_update",
    )(grad, turned, m, v)
    return new_first.transpose(1, 0, 2), new_second.transpose(1, 0, 2), update[None]


def solution(mesh):
    placed = (
        P("dp", "tensor"),
        P(),
        P("dp", "tensor"),
        P("tensor", "dp", None),
        P("tensor", "dp", None),
    )
    return jax.shard_map(
        on_device,
        mesh=mesh,
        in_specs=placed,
        out_specs=(P("tensor", "dp", None), P("tensor", "dp", None), P("tensor", "dp", None)),
        check_vma=False,
    )
```

```python
import functools

import jax
import jax.numpy as jnp
from jax import lax
from jax.experimental import pallas as pl
from jax.experimental.pallas import tpu as pltpu
from jax.sharding import PartitionSpec as P

STEP = 100
MESH = pl.DeviceIdType.MESH
F32 = jnp.float32
BF16 = jnp.bfloat16

NX, NZ, NY = 4, 12, 2
NYH, NC = 4, 2
OWN = 19
PAD = 20
QUADS = NZ // 4
TOK = 48
HALF = 128

TENSOR_PEERS = ((2, 0), (2, 1), (1, 0), (3, 0), (1, 1), (3, 1), (0, 1))
XY_PEERS = ((2, 1), (2, 0), (1, 1), (3, 1), (1, 0), (3, 0), (0, 1))
FIRST_ROUTES = (((1, 0), (1, 1)), ((3, 0), (3, 1)), ((1, 0), (1, 0)), ((3, 0), (3, 0)))
SECOND_ROUTES = tuple((p, p) for p in XY_PEERS)
MERGED = len(FIRST_ROUTES)
GROUPS = ((6, 5, 7, 4), (8, 3, 9, 2), (10, 1, 11, 0))


def reduce_kernel(
    act_hbm, basis_hbm, og_hbm, m_hbm, v_hbm,
    grad_out, turned_out, m_out, v_out,
    act, rows, basis, og, m_in, v_in,
    part, part_in, code, ogp, chunk, chunk_in, merged, acc, far_acc, far_send, far_in, far_sum, far_got, near_acc, near_send, near_in,
    load_sem, a_send, a_recv, g_send, g_recv, x_send, x_recv, f_send, f_recv, l_send, l_recv, z_send, z_recv, hello,
):
    dp, t = lax.axis_index("dp"), lax.axis_index("tensor")
    x, z, y = dp // (NZ * NY), lax.rem(dp // NY, NZ), lax.rem(dp, NY)
    yh, core = t // NC, lax.rem(t, NC)
    n_ten, n_xy = len(TENSOR_PEERS), len(XY_PEERS)

    def tensor_at(k):
        a, c = TENSOR_PEERS[k]
        return lax.rem(yh + a, NYH) * NC + lax.rem(core + c, NC)

    def xy_at(place):
        dx, dy = place
        return lax.rem(x + dx, NX), lax.rem(y + dy, NY)

    def dp_at(px, pz, py):
        return (lax.rem(px, NX) * NZ + lax.rem(pz, NZ)) * NY + lax.rem(py, NY)

    barrier = pltpu.get_barrier_semaphore()

    def signal(to_dp, to_t):
        pl.semaphore_signal(barrier, inc=1, device_id=(to_dp, to_t), device_id_type=MESH)

    for k in range(n_ten):
        signal(dp, tensor_at(k))
    for dz in (3, 9, 2, 10, 1, 11):
        signal(dp_at(x, z + dz, y), t)
    for dx, dy in XY_PEERS:
        signal(dp_at(x + dx, z, y + dy), t)

    tokens, feats = act.shape
    start = pl.multiple_of(t * feats, feats)
    n_cut = 4
    first_loads = []
    for i in range(n_cut):
        n = feats // n_cut
        first_loads.append(
            pltpu.make_async_copy(
                basis_hbm.at[pl.ds(start + i * n, n)], rows.at[pl.ds(i * n, n)], load_sem.at[i]
            )
        )
        n = tokens // n_cut
        first_loads.append(
            pltpu.make_async_copy(
                act_hbm.at[pl.ds(i * n, n)], act.at[pl.ds(i * n, n)], load_sem.at[n_cut + i]
            )
        )
    og_load = pltpu.make_async_copy(og_hbm, og, load_sem.at[2 * n_cut])
    m_load = pltpu.make_async_copy(m_hbm, m_in, load_sem.at[2 * n_cut + 1])
    v_load = pltpu.make_async_copy(v_hbm, v_in, load_sem.at[2 * n_cut + 2])
    basis_load = pltpu.make_async_copy(basis_hbm, basis, load_sem.at[2 * n_cut + 3])
    for load in first_loads:
        load.start()

    for load in first_loads:
        load.wait()
    og_load.start()
    m_load.start()
    v_load.start()
    basis_load.start()
    a_copies = []
    for h in range(2):
        coded = jnp.dot(act[...], rows[:, h * HALF : (h + 1) * HALF], preferred_element_type=F32)
        part[h] = coded.astype(BF16).reshape(part.shape[1:])
        if h == 0:
            pl.semaphore_wait(barrier, n_ten + 6 + n_xy)
            for i, dz in enumerate((3, NZ - 3)):
                pl.semaphore_signal(
                    hello.at[i], inc=1, device_id=(dp_at(x, z + dz, y), t), device_id_type=MESH
                )
        for k in range(n_ten):
            peer = tensor_at(k)
            copy = pltpu.make_async_remote_copy(
                src_ref=part.at[h, peer], dst_ref=part_in.at[h, k],
                send_sem=a_send.at[h, k], recv_sem=a_recv.at[h, k],
                device_id=(dp, peer), device_id_type=MESH,
            )
            copy.start()
            a_copies.append(copy)

    og_load.wait()
    unit_rows = NY * 4 * PAD
    n_out, n_in = QUADS * unit_rows, NZ * NY * OWN
    window = n_in + 8
    r = lax.broadcasted_iota(jnp.int32, (n_out, 1), 0)
    place, line = r // PAD, lax.rem(r, PAD)
    group, in_group = place // (NY * 4), lax.rem(place, NY * 4)
    ahead = jnp.zeros_like(r)
    for a in range(QUADS):
        for b in range(4):
            ahead = jnp.where((group == a) & (lax.rem(in_group, 4) == b), GROUPS[a][b], ahead)
    to_z = z + ahead
    to_z = jnp.where(to_z >= NZ, to_z - NZ, to_z)
    source = (to_z * NY + in_group // 4) * OWN + line
    source = jnp.where(line < OWN, source, -window)
    c = lax.broadcasted_iota(jnp.int32, (n_out, window), 1)
    picks = [jnp.where(c == source + shift, 1.0, 0.0).astype(BF16) for shift in (0, 8)]
    for ox in range(NX):
        shift = ox * n_in % 16
        first = ox * n_in - shift
        moved = jnp.dot(picks[shift // 8], og[first : first + window, :], preferred_element_type=F32).astype(BF16)
        for j in range(QUADS):
            ogp[j, ox * unit_rows : (ox + 1) * unit_rows, :] = moved[j * unit_rows : (j + 1) * unit_rows, :]
    far_acc[...] = jnp.zeros_like(far_acc)
    near_acc[...] = jnp.zeros_like(near_acc)

    g_copies = []
    for h in range(2):
        total = part[h, t].astype(F32)
        for k in range(n_ten):
            a_copies[h * n_ten + k].wait_recv()
            total = total + part_in[h, k].astype(F32)
        code[h, t] = total.astype(BF16)
        for k in range(n_ten):
            copy = pltpu.make_async_remote_copy(
                src_ref=code.at[h, t], dst_ref=code.at[h, t],
                send_sem=g_send.at[h, k], recv_sem=g_recv.at[h, k],
                device_id=(dp, tensor_at(k)), device_id_type=MESH,
            )
            copy.start()
            g_copies.append(copy)

    m_load.wait()
    v_load.wait()
    m_out[...] = jnp.zeros_like(m_out)
    v_out[...] = jnp.ones_like(v_out)
    for i in range(OWN):
        m_out[i : i + 1, :] = m_in[i]
        v_out[i : i + 1, :] = v_in[i]
    basis_load.wait()
    wide = 1024
    for i in range(basis.shape[0] // wide):
        turned_out[:, i * wide : (i + 1) * wide] = basis[i * wide : (i + 1) * wide, :].T

    def along_z(src, dst, send_sem, recv_sem):
        copies = []
        for j, group in enumerate(GROUPS):
            copies.append([])
            for zz, ahead in enumerate(group):
                if ahead:
                    copies[j].append(
                        pltpu.make_async_remote_copy(
                            src_ref=src.at[j, zz], dst_ref=dst.at[ahead - 1],
                            send_sem=send_sem.at[ahead - 1], recv_sem=recv_sem.at[ahead - 1],
                            device_id=(dp_at(x, z + ahead, y), t), device_id_type=MESH,
                        )
                    )
        return copies

    def sum_along_z(src, copies):
        total = src[QUADS - 1, 3].astype(F32)
        for group, sent in zip(GROUPS, copies):
            for ahead, copy in zip(group, sent):
                copy.wait_recv()
                total = total + copy.dst_ref[...].astype(F32)
        return total

    far_copies = along_z(far_send, far_in, f_send, f_recv)
    near_copies = along_z(near_send, near_in, z_send, z_recv)
    two_x = lax.rem(x + 2, NX)
    far_rows = pl.ds(pl.multiple_of(two_x * unit_rows, unit_rows), unit_rows)
    x_copies = [[] for _ in range(2 * QUADS)]
    for h in range(2):
        for k in range(n_ten):
            g_copies[h * n_ten + k].wait_recv()
        coded = code[h].reshape((n_ten + 1) * TOK, HALF)
        for j in range(QUADS):
            at = h * QUADS + j
            term = jnp.dot(ogp[j], coded, preferred_element_type=F32)
            chunk[at] = term.astype(BF16).reshape(chunk.shape[1:])
            for k, (to, share) in enumerate(SECOND_ROUTES if h else FIRST_ROUTES):
                px, py = xy_at(to)
                sx, sy = xy_at(share)
                copy = pltpu.make_async_remote_copy(
                    src_ref=chunk.at[at, sx * NY + sy], dst_ref=chunk_in.at[at, k],
                    send_sem=x_send.at[at, k], recv_sem=x_recv.at[at, k],
                    device_id=((px * NZ + z) * NY + py, t), device_id_type=MESH,
                )
                copy.start()
                x_copies[at].append(copy)
        if h == 0:
            for i in range(2):
                pl.semaphore_wait(hello.at[i], 1)
            for j in range(QUADS):
                acc[...] = jnp.dot(ogp[j, far_rows, :], coded, preferred_element_type=F32)
                for zz in range(4):
                    for py in range(NY):
                        at = (py * 4 + zz) * PAD
                        far_acc[j, zz, 24 * py : 24 * py + PAD, :] = acc[at : at + PAD, :]
                    far_send[j, zz] = far_acc[j, zz].astype(BF16)
                for copy in far_copies[j]:
                    copy.start()

    for j in range(QUADS):
        total = chunk[j, x * NY + 1 - y].astype(F32)
        for k in range(2):
            x_copies[j][k].wait_recv()
            total = total + chunk_in[j, k].astype(F32)
        merged[j] = total.astype(BF16)
        copy = pltpu.make_async_remote_copy(
            src_ref=merged.at[j], dst_ref=chunk_in.at[j, MERGED],
            send_sem=x_send.at[j, MERGED], recv_sem=x_recv.at[j, MERGED],
            device_id=(dp_at(x, z, y + 1), t), device_id_type=MESH,
        )
        copy.start()
        x_copies[j].append(copy)
    two_copies = []
    for j in range(QUADS):
        if j == QUADS - 1:
            total = sum_along_z(far_send, far_copies)
            blank = jnp.zeros((8, HALF), F32)
            for py in range(NY):
                far_sum[py] = jnp.concatenate([total[24 * py : 24 * py + 24], blank], axis=0).astype(BF16)
                copy = pltpu.make_async_remote_copy(
                    src_ref=far_sum.at[py], dst_ref=far_got.at[y], send_sem=l_send.at[py], recv_sem=l_recv.at[y],
                    device_id=(dp_at(x + 2, z, py), t), device_id_type=MESH,
                )
                copy.start()
                two_copies.append(copy)
        for h in range(2):
            at = h * QUADS + j
            total = chunk[at, x * NY + y].astype(F32)
            for k in range(0 if h else 2, len(x_copies[at])):
                x_copies[at][k].wait_recv()
                total = total + chunk_in[at, k].astype(F32)
            acc[0 : 4 * PAD, :] = total
            for zz in range(4):
                near_acc[j, zz, 24 * h : 24 * h + PAD, :] = acc[zz * PAD : (zz + 1) * PAD, :]
        for zz in range(4):
            near_send[j, zz] = near_acc[j, zz].astype(BF16)
        for copy in near_copies[j]:
            copy.start()

    first = jnp.zeros((24, HALF), F32)
    for py in range(NY):
        pltpu.make_async_copy(far_got.at[py], far_got.at[py], l_recv.at[py]).wait()
        first = first + far_got[py].astype(F32)[0:24]
    total = sum_along_z(near_send, near_copies)
    grad_out[...] = jnp.concatenate([total[0:24] + first, total[24:48]], axis=1)
    z_copies = two_copies + sum(far_copies + near_copies + x_copies, [])
    for copy in a_copies + g_copies + z_copies:
        copy.wait_send()


def step_kernel(grad, turned, m, v, m_hbm, v_hbm, upd_hbm, m_rows, v_rows, upd, sem):
    g = grad[...]
    new_first = 0.9 * m[...] + 0.1 * g
    new_second = 0.999 * v[...] + 0.001 * g * g
    first_hat = new_first / (1.0 - 0.9**STEP)
    second_hat = new_second / (1.0 - 0.999**STEP)
    direction = first_hat / (jnp.sqrt(second_hat) + 1e-08)
    direction = jnp.concatenate([direction, jnp.zeros((8, direction.shape[1]), F32)], axis=0).astype(BF16)
    wide = 2048
    saves = []
    for i in range(turned.shape[1] // wide):
        cols = pl.ds(i * wide, wide)
        upd[:, cols] = jnp.dot(direction, turned[:, cols], preferred_element_type=F32)[:OWN].astype(BF16)
        save = pltpu.make_async_copy(upd.at[:, cols], upd_hbm.at[:, cols], sem.at[i])
        save.start()
        saves.append(save)
    for i in range(OWN):
        m_rows[i] = new_first[i : i + 1, :]
        v_rows[i] = new_second[i : i + 1, :]
    saves.append(pltpu.make_async_copy(m_rows, m_hbm, sem.at[4]))
    saves.append(pltpu.make_async_copy(v_rows, v_hbm, sem.at[5]))
    saves[-2].start()
    saves[-1].start()
    for save in saves:
        save.wait()


def on_device(activations, basis, out_grad, first_moment, second_moment):
    d, rank = basis.shape
    tokens, feats = activations.shape
    units = out_grad.shape[1]
    hbm = pl.BlockSpec(memory_space=pltpu.HBM)
    vmem = pl.BlockSpec(memory_space=pltpu.VMEM)
    dma = pltpu.SemaphoreType.DMA
    n_ten, n_xy = len(TENSOR_PEERS), len(XY_PEERS)
    steps = 2 * QUADS
    grad, turned, m, v = pl.pallas_call(
        reduce_kernel,
        out_shape=(
            jax.ShapeDtypeStruct((24, rank), F32),
            jax.ShapeDtypeStruct((rank, d), BF16),
            jax.ShapeDtypeStruct((24, rank), F32),
            jax.ShapeDtypeStruct((24, rank), F32),
        ),
        in_specs=[hbm] * 5,
        out_specs=(vmem,) * 4,
        scratch_shapes=[
            pltpu.VMEM((tokens, feats), BF16),
            pltpu.VMEM((feats, rank), BF16),
            pltpu.VMEM((d, rank), BF16),
            pltpu.VMEM((units, tokens), BF16),
            pltpu.VMEM((OWN, 1, rank), F32),
            pltpu.VMEM((OWN, 1, rank), F32),
            pltpu.VMEM((2, n_ten + 1, TOK, HALF), BF16),
            pltpu.VMEM((2, n_ten, TOK, HALF), BF16),
            pltpu.VMEM((2, n_ten + 1, TOK, HALF), BF16),
            pltpu.VMEM((QUADS, NX * NY * 4 * PAD, tokens), BF16),
            pltpu.VMEM((steps, NX * NY, 4 * PAD, HALF), BF16),
            pltpu.VMEM((steps, n_xy, 4 * PAD, HALF), BF16),
            pltpu.VMEM((QUADS, 4 * PAD, HALF), BF16),
            pltpu.VMEM((NY * 4 * PAD, HALF), F32),
            pltpu.VMEM((QUADS, 4, 48, HALF), F32),
            pltpu.VMEM((QUADS, 4, 48, HALF), BF16),
            pltpu.VMEM((NZ - 1, 48, HALF), BF16),
            pltpu.VMEM((NY, 32, HALF), BF16),
            pltpu.VMEM((NY, 32, HALF), BF16),
            pltpu.VMEM((QUADS, 4, 48, HALF), F32),
            pltpu.VMEM((QUADS, 4, 48, HALF), BF16),
            pltpu.VMEM((NZ - 1, 48, HALF), BF16),
            dma((12,)),
            dma((2, n_ten)),
            dma((2, n_ten)),
            dma((2, n_ten)),
            dma((2, n_ten)),
            dma((steps, n_xy)),
            dma((steps, n_xy)),
            dma((NZ - 1,)),
            dma((NZ - 1,)),
            dma((NY,)),
            dma((NY,)),
            dma((NZ - 1,)),
            dma((NZ - 1,)),
            pltpu.SemaphoreType.REGULAR((2,)),
        ],
        compiler_params=pltpu.CompilerParams(
            collective_id=0, has_side_effects=True, vmem_limit_bytes=40 << 20
        ),
        name="reduce_gradient",
    )(*[
        pltpu.with_memory_space_constraint(a, pltpu.HBM)
        for a in (
            activations,
            basis,
            out_grad.T,
            first_moment.transpose(1, 0, 2),
            second_moment.transpose(1, 0, 2),
        )
    ])
    new_first, new_second, update = pl.pallas_call(
        step_kernel,
        out_shape=(
            jax.ShapeDtypeStruct((OWN, 1, rank), F32),
            jax.ShapeDtypeStruct((OWN, 1, rank), F32),
            jax.ShapeDtypeStruct((OWN, d), BF16),
        ),
        in_specs=[vmem] * 4,
        out_specs=(hbm,) * 3,
        scratch_shapes=[
            pltpu.VMEM((OWN, 1, rank), F32),
            pltpu.VMEM((OWN, 1, rank), F32),
            pltpu.VMEM((OWN, d), BF16),
            dma((6,)),
        ],
        compiler_params=pltpu.CompilerParams(vmem_limit_bytes=16 << 20),
        name="adam_update",
    )(grad, turned, m, v)
    return new_first.transpose(1, 0, 2), new_second.transpose(1, 0, 2), update[None]


def solution(mesh):
    placed = (
        P("dp", "tensor"),
        P(),
        P("dp", "tensor"),
        P("tensor", "dp", None),
        P("tensor", "dp", None),
    )
    return jax.shard_map(
        on_device,
        mesh=mesh,
        in_specs=placed,
        out_specs=(P("tensor", "dp", None), P("tensor", "dp", None), P("tensor", "dp", None)),
        check_vma=False,
    )
```

```python
import functools

import jax
import jax.numpy as jnp
from jax import lax
from jax.experimental import pallas as pl
from jax.experimental.pallas import tpu as pltpu
from jax.sharding import PartitionSpec as P

STEP = 100
MESH = pl.DeviceIdType.MESH
F32 = jnp.float32
BF16 = jnp.bfloat16

NX, NZ, NY = 4, 12, 2
NYH, NC = 4, 2
OWN = 19
PAD = 20
QUADS = NZ // 4
TOK = 48
HALF = 128

TENSOR_PEERS = ((2, 0), (2, 1), (1, 0), (3, 0), (1, 1), (3, 1), (0, 1))
XY_PEERS = ((2, 1), (2, 0), (1, 1), (3, 1), (1, 0), (3, 0), (0, 1))


def reduce_kernel(
    act_hbm, basis_hbm, og_hbm, m_hbm, v_hbm,
    grad_out, turned_out, m_out, v_out,
    act, rows, basis, og, m_in, v_in,
    part, part_in, code, ogp, chunk, chunk_in, acc, cut, z_out, z_in,
    load_sem, a_send, a_recv, g_send, g_recv, x_send, x_recv, z_send, z_recv, hello,
):
    dp, t = lax.axis_index("dp"), lax.axis_index("tensor")
    x, z, y = dp // (NZ * NY), lax.rem(dp // NY, NZ), lax.rem(dp, NY)
    yh, core = t // NC, lax.rem(t, NC)
    n_ten, n_xy = len(TENSOR_PEERS), len(XY_PEERS)

    def tensor_at(k):
        a, c = TENSOR_PEERS[k]
        return lax.rem(yh + a, NYH) * NC + lax.rem(core + c, NC)

    def xy_at(place):
        dx, dy = place
        return lax.rem(x + dx, NX), lax.rem(y + dy, NY)

    def dp_at(px, pz, py):
        return (lax.rem(px, NX) * NZ + lax.rem(pz, NZ)) * NY + lax.rem(py, NY)

    barrier = pltpu.get_barrier_semaphore()

    def signal(to_dp, to_t):
        pl.semaphore_signal(barrier, inc=1, device_id=(to_dp, to_t), device_id_type=MESH)

    for k in range(n_ten):
        signal(dp, tensor_at(k))
    for dx, dy in XY_PEERS:
        signal(dp_at(x + dx, z, y + dy), t)
    for to in range(NZ - 1, 0, -1):

        @pl.when(z < to)
        def _():
            signal(dp_at(x, to, y), t)

    tokens, feats = act.shape
    start = pl.multiple_of(t * feats, feats)
    n_cut = 4
    first_loads = []
    for i in range(n_cut):
        n = feats // n_cut
        first_loads.append(
            pltpu.make_async_copy(
                basis_hbm.at[pl.ds(start + i * n, n)], rows.at[pl.ds(i * n, n)], load_sem.at[i]
            )
        )
        n = tokens // n_cut
        first_loads.append(
            pltpu.make_async_copy(
                act_hbm.at[pl.ds(i * n, n)], act.at[pl.ds(i * n, n)], load_sem.at[n_cut + i]
            )
        )
    og_load = pltpu.make_async_copy(og_hbm, og, load_sem.at[2 * n_cut])
    m_load = pltpu.make_async_copy(m_hbm, m_in, load_sem.at[2 * n_cut + 1])
    v_load = pltpu.make_async_copy(v_hbm, v_in, load_sem.at[2 * n_cut + 2])
    basis_load = pltpu.make_async_copy(basis_hbm, basis, load_sem.at[2 * n_cut + 3])
    for load in first_loads:
        load.start()

    for load in first_loads:
        load.wait()
    og_load.start()
    m_load.start()
    v_load.start()
    basis_load.start()
    a_copies = []
    for h in range(2):
        coded = jnp.dot(act[...], rows[:, h * HALF : (h + 1) * HALF], preferred_element_type=F32)
        part[h] = coded.astype(BF16).reshape(part.shape[1:])
        if h == 0:
            pl.semaphore_wait(barrier, n_ten + n_xy + z)
        for k in range(n_ten):
            peer = tensor_at(k)
            copy = pltpu.make_async_remote_copy(
                src_ref=part.at[h, peer], dst_ref=part_in.at[h, k],
                send_sem=a_send.at[h, k], recv_sem=a_recv.at[h, k],
                device_id=(dp, peer), device_id_type=MESH,
            )
            copy.start()
            a_copies.append(copy)

    for to in range(NZ - 1):

        @pl.when(z > to)
        def _():
            pl.semaphore_signal(hello.at[z], inc=1, device_id=(dp_at(x, to, y), t), device_id_type=MESH)

    og_load.wait()
    n_out, n_in = 16 * PAD, 16 * OWN
    unit_rows = 8 * PAD
    r = lax.broadcasted_iota(jnp.int32, (n_out, n_in), 0)
    c = lax.broadcasted_iota(jnp.int32, (n_out, n_in), 1)
    unit, in_unit = r // unit_rows, lax.rem(r, unit_rows)
    place, line = in_unit // PAD, lax.rem(in_unit, PAD)
    owner = unit * 8 + lax.rem(place, 4) * 2 + place // 4
    pick = jnp.where((line < OWN) & (c == owner * OWN + line), 1.0, 0.0).astype(BF16)
    for b in range(NX * NZ * NY // 16):
        moved = jnp.dot(pick, og[b * n_in : (b + 1) * n_in, :], preferred_element_type=F32).astype(BF16)
        for i in range(2):
            ox, oq = (2 * b + i) // QUADS, (2 * b + i) % QUADS
            ogp[oq, ox * unit_rows : (ox + 1) * unit_rows, :] = moved[i * unit_rows : (i + 1) * unit_rows, :]
    cut[...] = jnp.zeros_like(cut)

    g_copies = []
    for h in range(2):
        total = part[h, t].astype(F32)
        for k in range(n_ten):
            a_copies[h * n_ten + k].wait_recv()
            total = total + part_in[h, k].astype(F32)
        code[h, t] = total.astype(BF16)
        for k in range(n_ten):
            copy = pltpu.make_async_remote_copy(
                src_ref=code.at[h, t], dst_ref=code.at[h, t],
                send_sem=g_send.at[h, k], recv_sem=g_recv.at[h, k],
                device_id=(dp, tensor_at(k)), device_id_type=MESH,
            )
            copy.start()
            g_copies.append(copy)

    m_load.wait()
    v_load.wait()
    m_out[...] = jnp.zeros_like(m_out)
    v_out[...] = jnp.ones_like(v_out)
    for i in range(OWN):
        m_out[i : i + 1, :] = m_in[i]
        v_out[i : i + 1, :] = v_in[i]
    basis_load.wait()
    wide = 1024
    for i in range(basis.shape[0] // wide):
        turned_out[:, i * wide : (i + 1) * wide] = basis[i * wide : (i + 1) * wide, :].T

    def z_copy(to):
        return pltpu.make_async_remote_copy(
            src_ref=z_out.at[to], dst_ref=z_in.at[z], send_sem=z_send.at[to], recv_sem=z_recv.at[z],
            device_id=(dp_at(x, to, y), t), device_id_type=MESH,
        )

    x_copies = {}

    def share(h, q):
        coded = code[h].reshape((n_ten + 1) * TOK, HALF)
        at = h * QUADS + q
        term = jnp.dot(ogp[q], coded, preferred_element_type=F32)
        chunk[at] = term.astype(BF16).reshape(chunk.shape[1:])
        x_copies[at] = []
        for k in range(n_xy):
            px, py = xy_at(XY_PEERS[k])
            copy = pltpu.make_async_remote_copy(
                src_ref=chunk.at[at, px * NY + py], dst_ref=chunk_in.at[at, k],
                send_sem=x_send.at[at, k], recv_sem=x_recv.at[at, k],
                device_id=((px * NZ + z) * NY + py, t), device_id_type=MESH,
            )
            copy.start()
            x_copies[at].append(copy)

    def collect(q):
        for h in range(2):
            at = h * QUADS + q
            total = chunk[at, x * NY + y].astype(F32)
            for k in range(n_xy):
                x_copies[at][k].wait_recv()
                total = total + chunk_in[at, k].astype(F32)
            acc[...] = total
            for zz in range(4):
                cut[zz, 24 * h : 24 * h + PAD, :] = acc[zz * PAD : (zz + 1) * PAD, :]
        for zz in range(4):
            to = 4 * q + zz
            z_out[to] = cut[zz].astype(BF16)

            @pl.when(z < to)
            def _():
                pl.semaphore_wait(hello.at[to], 1)

            @pl.when(z != to)
            def _():
                z_copy(to).start()

    for h in range(2):
        for k in range(n_ten):
            g_copies[h * n_ten + k].wait_recv()
        share(h, 0)
    share(0, 1)
    for q in range(QUADS):
        collect(q)
        if q + 1 < QUADS:
            share(1, q + 1)
        if q + 2 < QUADS:
            share(0, q + 2)

    total = z_out[z].astype(F32)
    for ahead in range(1, NZ):
        sender = lax.rem(z + ahead, NZ)
        pltpu.make_async_copy(z_in.at[sender], z_in.at[sender], z_recv.at[sender]).wait()
        total = total + z_in[sender].astype(F32)
    grad_out[...] = jnp.concatenate([total[0:24], total[24:48]], axis=1)
    for to in range(NZ):

        @pl.when(z != to)
        def _():
            z_copy(to).wait_send()

    for copy in a_copies + g_copies + sum(x_copies.values(), []):
        copy.wait_send()


def step_kernel(grad, turned, m, v, m_hbm, v_hbm, upd_hbm, m_rows, v_rows, upd, sem):
    g = grad[...]
    new_first = 0.9 * m[...] + 0.1 * g
    new_second = 0.999 * v[...] + 0.001 * g * g
    first_hat = new_first / (1.0 - 0.9**STEP)
    second_hat = new_second / (1.0 - 0.999**STEP)
    direction = first_hat / (jnp.sqrt(second_hat) + 1e-08)
    direction = jnp.concatenate([direction, jnp.zeros((8, direction.shape[1]), F32)], axis=0).astype(BF16)
    wide = 2048
    saves = []
    for i in range(turned.shape[1] // wide):
        cols = pl.ds(i * wide, wide)
        upd[:, cols] = jnp.dot(direction, turned[:, cols], preferred_element_type=F32)[:OWN].astype(BF16)
        save = pltpu.make_async_copy(upd.at[:, cols], upd_hbm.at[:, cols], sem.at[i])
        save.start()
        saves.append(save)
    for i in range(OWN):
        m_rows[i] = new_first[i : i + 1, :]
        v_rows[i] = new_second[i : i + 1, :]
    saves.append(pltpu.make_async_copy(m_rows, m_hbm, sem.at[4]))
    saves.append(pltpu.make_async_copy(v_rows, v_hbm, sem.at[5]))
    saves[-2].start()
    saves[-1].start()
    for save in saves:
        save.wait()


def on_device(activations, basis, out_grad, first_moment, second_moment):
    d, rank = basis.shape
    tokens, feats = activations.shape
    units = out_grad.shape[1]
    hbm = pl.BlockSpec(memory_space=pltpu.HBM)
    vmem = pl.BlockSpec(memory_space=pltpu.VMEM)
    dma = pltpu.SemaphoreType.DMA
    n_ten, n_xy = len(TENSOR_PEERS), len(XY_PEERS)
    steps = 2 * QUADS
    grad, turned, m, v = pl.pallas_call(
        reduce_kernel,
        out_shape=(
            jax.ShapeDtypeStruct((24, rank), F32),
            jax.ShapeDtypeStruct((rank, d), BF16),
            jax.ShapeDtypeStruct((24, rank), F32),
            jax.ShapeDtypeStruct((24, rank), F32),
        ),
        in_specs=[hbm] * 5,
        out_specs=(vmem,) * 4,
        scratch_shapes=[
            pltpu.VMEM((tokens, feats), BF16),
            pltpu.VMEM((feats, rank), BF16),
            pltpu.VMEM((d, rank), BF16),
            pltpu.VMEM((units, tokens), BF16),
            pltpu.VMEM((OWN, 1, rank), F32),
            pltpu.VMEM((OWN, 1, rank), F32),
            pltpu.VMEM((2, n_ten + 1, TOK, HALF), BF16),
            pltpu.VMEM((2, n_ten, TOK, HALF), BF16),
            pltpu.VMEM((2, n_ten + 1, TOK, HALF), BF16),
            pltpu.VMEM((QUADS, NX * NY * 4 * PAD, tokens), BF16),
            pltpu.VMEM((steps, NX * NY, 4 * PAD, HALF), BF16),
            pltpu.VMEM((steps, n_xy, 4 * PAD, HALF), BF16),
            pltpu.VMEM((4 * PAD, HALF), F32),
            pltpu.VMEM((4, 48, HALF), F32),
            pltpu.VMEM((NZ, 48, HALF), BF16),
            pltpu.VMEM((NZ, 48, HALF), BF16),
            dma((12,)),
            dma((2, n_ten)),
            dma((2, n_ten)),
            dma((2, n_ten)),
            dma((2, n_ten)),
            dma((steps, n_xy)),
            dma((steps, n_xy)),
            dma((NZ,)),
            dma((NZ,)),
            pltpu.SemaphoreType.REGULAR((NZ,)),
        ],
        compiler_params=pltpu.CompilerParams(
            collective_id=0, has_side_effects=True, vmem_limit_bytes=40 << 20
        ),
        name="reduce_gradient",
    )(*[
        pltpu.with_memory_space_constraint(a, pltpu.HBM)
        for a in (
            activations,
            basis,
            out_grad.T,
            first_moment.transpose(1, 0, 2),
            second_moment.transpose(1, 0, 2),
        )
    ])
    new_first, new_second, update = pl.pallas_call(
        step_kernel,
        out_shape=(
            jax.ShapeDtypeStruct((OWN, 1, rank), F32),
            jax.ShapeDtypeStruct((OWN, 1, rank), F32),
            jax.ShapeDtypeStruct((OWN, d), BF16),
        ),
        in_specs=[vmem] * 4,
        out_specs=(hbm,) * 3,
        scratch_shapes=[
            pltpu.VMEM((OWN, 1, rank), F32),
            pltpu.VMEM((OWN, 1, rank), F32),
            pltpu.VMEM((OWN, d), BF16),
            dma((6,)),
        ],
        compiler_params=pltpu.CompilerParams(vmem_limit_bytes=16 << 20),
        name="adam_update",
    )(grad, turned, m, v)
    return new_first.transpose(1, 0, 2), new_second.transpose(1, 0, 2), update[None]


def solution(mesh):
    placed = (
        P("dp", "tensor"),
        P(),
        P("dp", "tensor"),
        P("tensor", "dp", None),
        P("tensor", "dp", None),
    )
    return jax.shard_map(
        on_device,
        mesh=mesh,
        in_specs=placed,
        out_specs=(P("tensor", "dp", None), P("tensor", "dp", None), P("tensor", "dp", None)),
        check_vma=False,
    )
```

```python
import functools

import jax
import jax.numpy as jnp
from jax import lax
from jax.experimental import pallas as pl
from jax.experimental.pallas import tpu as pltpu
from jax.sharding import PartitionSpec as P

STEP = 100
MESH = pl.DeviceIdType.MESH
F32 = jnp.float32
BF16 = jnp.bfloat16

NX, NZ, NY = 4, 12, 2
NYH, NC = 4, 2
OWN = 19
PAD = 20
SIZES = (1, 3, 4, 4)
ROWS = (32, 64, 80, 80)
STARTS = (0, 1, 4, 8)
FIRST_ROW = (0, 32, 96, 176)
ALL_ROWS = 256
TOK = 48
HALF = 128

TENSOR_PEERS = ((2, 0), (2, 1), (1, 0), (3, 0), (1, 1), (3, 1), (0, 1))
XY_PEERS = ((2, 1), (2, 0), (1, 1), (3, 1), (1, 0), (3, 0), (0, 1))


def reduce_kernel(
    act_hbm, basis_hbm, og_hbm, m_hbm, v_hbm,
    grad_out, turned_out, m_out, v_out,
    act, rows, basis, og, m_in, v_in,
    part, part_in, code, ogp, chunk, chunk_in, acc, cut, z_out, z_in,
    load_sem, a_send, a_recv, g_send, g_recv, x_send, x_recv, z_send, z_recv, hello,
):
    dp, t = lax.axis_index("dp"), lax.axis_index("tensor")
    x, z, y = dp // (NZ * NY), lax.rem(dp // NY, NZ), lax.rem(dp, NY)
    yh, core = t // NC, lax.rem(t, NC)
    n_ten, n_xy = len(TENSOR_PEERS), len(XY_PEERS)

    def tensor_at(k):
        a, c = TENSOR_PEERS[k]
        return lax.rem(yh + a, NYH) * NC + lax.rem(core + c, NC)

    def xy_at(place):
        dx, dy = place
        return lax.rem(x + dx, NX), lax.rem(y + dy, NY)

    def dp_at(px, pz, py):
        return (lax.rem(px, NX) * NZ + lax.rem(pz, NZ)) * NY + lax.rem(py, NY)

    barrier = pltpu.get_barrier_semaphore()

    def signal(to_dp, to_t):
        pl.semaphore_signal(barrier, inc=1, device_id=(to_dp, to_t), device_id_type=MESH)

    for k in range(n_ten):
        signal(dp, tensor_at(k))
    for dx, dy in XY_PEERS:
        signal(dp_at(x + dx, z, y + dy), t)
    for to in range(NZ - 1, 0, -1):

        @pl.when(z < to)
        def _():
            signal(dp_at(x, to, y), t)

    tokens, feats = act.shape
    start = pl.multiple_of(t * feats, feats)
    n_cut = 4
    first_loads = []
    for i in range(n_cut):
        n = feats // n_cut
        first_loads.append(
            pltpu.make_async_copy(
                basis_hbm.at[pl.ds(start + i * n, n)], rows.at[pl.ds(i * n, n)], load_sem.at[i]
            )
        )
        n = tokens // n_cut
        first_loads.append(
            pltpu.make_async_copy(
                act_hbm.at[pl.ds(i * n, n)], act.at[pl.ds(i * n, n)], load_sem.at[n_cut + i]
            )
        )
    og_load = pltpu.make_async_copy(og_hbm, og, load_sem.at[2 * n_cut])
    m_load = pltpu.make_async_copy(m_hbm, m_in, load_sem.at[2 * n_cut + 1])
    v_load = pltpu.make_async_copy(v_hbm, v_in, load_sem.at[2 * n_cut + 2])
    basis_load = pltpu.make_async_copy(basis_hbm, basis, load_sem.at[2 * n_cut + 3])
    for load in first_loads:
        load.start()

    for load in first_loads:
        load.wait()
    og_load.start()
    m_load.start()
    v_load.start()
    basis_load.start()
    a_copies = []
    for h in range(2):
        coded = jnp.dot(act[...], rows[:, h * HALF : (h + 1) * HALF], preferred_element_type=F32)
        part[h] = coded.astype(BF16).reshape(part.shape[1:])
        if h == 0:
            pl.semaphore_wait(barrier, n_ten + n_xy + z)
        for k in range(n_ten):
            peer = tensor_at(k)
            copy = pltpu.make_async_remote_copy(
                src_ref=part.at[h, peer], dst_ref=part_in.at[h, k],
                send_sem=a_send.at[h, k], recv_sem=a_recv.at[h, k],
                device_id=(dp, peer), device_id_type=MESH,
            )
            copy.start()
            a_copies.append(copy)

    for to in range(NZ - 1):

        @pl.when(z > to)
        def _():
            pl.semaphore_signal(hello.at[z], inc=1, device_id=(dp_at(x, to, y), t), device_id_type=MESH)

    og_load.wait()
    n_in = NZ * NY * OWN
    window = n_in + 8
    r = lax.broadcasted_iota(jnp.int32, (NY * ALL_ROWS, 1), 0)
    to_y, row = r // ALL_ROWS, lax.rem(r, ALL_ROWS)
    source = jnp.full_like(r, -window)
    for g in range(len(SIZES)):
        for i in range(SIZES[g]):
            at = FIRST_ROW[g] + i * PAD
            inside = (row >= at) & (row < at + OWN)
            source = jnp.where(inside, ((STARTS[g] + i) * NY + to_y) * OWN + row - at, source)
    c = lax.broadcasted_iota(jnp.int32, (NY * ALL_ROWS, window), 1)
    picks = [jnp.where(c == source + shift, 1.0, 0.0).astype(BF16) for shift in (0, 8)]
    for ox in range(NX):
        shift = ox * n_in % 16
        first = ox * n_in - shift
        moved = jnp.dot(picks[shift // 8], og[first : first + window, :], preferred_element_type=F32)
        ogp[ox * NY : (ox + 1) * NY] = moved.astype(BF16).reshape(NY, ALL_ROWS, moved.shape[1])
    cut[...] = jnp.zeros_like(cut)

    g_copies = []
    for h in range(2):
        total = part[h, t].astype(F32)
        for k in range(n_ten):
            a_copies[h * n_ten + k].wait_recv()
            total = total + part_in[h, k].astype(F32)
        code[h, t] = total.astype(BF16)
        for k in range(n_ten):
            copy = pltpu.make_async_remote_copy(
                src_ref=code.at[h, t], dst_ref=code.at[h, t],
                send_sem=g_send.at[h, k], recv_sem=g_recv.at[h, k],
                device_id=(dp, tensor_at(k)), device_id_type=MESH,
            )
            copy.start()
            g_copies.append(copy)

    m_load.wait()
    v_load.wait()
    m_out[...] = jnp.zeros_like(m_out)
    v_out[...] = jnp.ones_like(v_out)
    for i in range(OWN):
        m_out[i : i + 1, :] = m_in[i]
        v_out[i : i + 1, :] = v_in[i]
    basis_load.wait()
    wide = 1024
    for i in range(basis.shape[0] // wide):
        turned_out[:, i * wide : (i + 1) * wide] = basis[i * wide : (i + 1) * wide, :].T

    def z_copy(to):
        return pltpu.make_async_remote_copy(
            src_ref=z_out.at[to], dst_ref=z_in.at[z], send_sem=z_send.at[to], recv_sem=z_recv.at[z],
            device_id=(dp_at(x, to, y), t), device_id_type=MESH,
        )

    x_copies = {}

    def share(h, g):
        coded = code[h].reshape((n_ten + 1) * TOK, HALF)
        at, n = h * len(SIZES) + g, ROWS[g]
        rows_of = ogp[:, FIRST_ROW[g] : FIRST_ROW[g] + n, :].reshape(NX * NY * n, ogp.shape[2])
        term = jnp.dot(rows_of, coded, preferred_element_type=F32)
        chunk[at, :, 0:n, :] = term.astype(BF16).reshape(NX * NY, n, HALF)
        x_copies[at] = []
        for k in range(n_xy):
            px, py = xy_at(XY_PEERS[k])
            copy = pltpu.make_async_remote_copy(
                src_ref=chunk.at[at, px * NY + py, pl.ds(0, n)], dst_ref=chunk_in.at[at, k, pl.ds(0, n)],
                send_sem=x_send.at[at, k], recv_sem=x_recv.at[at, k],
                device_id=((px * NZ + z) * NY + py, t), device_id_type=MESH,
            )
            copy.start()
            x_copies[at].append(copy)

    def collect(g):
        n = ROWS[g]
        for h in range(2):
            at = h * len(SIZES) + g
            total = chunk[at, x * NY + y, 0:n, :].astype(F32)
            for k in range(n_xy):
                x_copies[at][k].wait_recv()
                total = total + chunk_in[at, k, 0:n, :].astype(F32)
            acc[0:n, :] = total
            for i in range(SIZES[g]):
                cut[i, 24 * h : 24 * h + PAD, :] = acc[i * PAD : (i + 1) * PAD, :]
        for i in range(SIZES[g]):
            to = STARTS[g] + i
            z_out[to] = cut[i].astype(BF16)

            @pl.when(z < to)
            def _():
                pl.semaphore_wait(hello.at[to], 1)

            @pl.when(z != to)
            def _():
                z_copy(to).start()

    for h in range(2):
        for k in range(n_ten):
            g_copies[h * n_ten + k].wait_recv()
        share(h, 0)
    share(0, 1)
    for g in range(len(SIZES)):
        collect(g)
        if g + 1 < len(SIZES):
            share(1, g + 1)
        if g + 2 < len(SIZES):
            share(0, g + 2)
    total = z_out[z].astype(F32)
    for ahead in range(1, NZ):
        sender = lax.rem(z + ahead, NZ)
        pltpu.make_async_copy(z_in.at[sender], z_in.at[sender], z_recv.at[sender]).wait()
        total = total + z_in[sender].astype(F32)
    grad_out[...] = jnp.concatenate([total[0:24], total[24:48]], axis=1)
    for to in range(NZ):

        @pl.when(z != to)
        def _():
            z_copy(to).wait_send()

    for copy in a_copies + g_copies + sum(x_copies.values(), []):
        copy.wait_send()


def step_kernel(grad, turned, m, v, m_hbm, v_hbm, upd_hbm, m_rows, v_rows, upd, sem):
    g = grad[...]
    new_first = 0.9 * m[...] + 0.1 * g
    new_second = 0.999 * v[...] + 0.001 * g * g
    first_hat = new_first / (1.0 - 0.9**STEP)
    second_hat = new_second / (1.0 - 0.999**STEP)
    direction = first_hat / (jnp.sqrt(second_hat) + 1e-08)
    direction = jnp.concatenate([direction, jnp.zeros((8, direction.shape[1]), F32)], axis=0).astype(BF16)
    wide = 2048
    saves = []
    for i in range(turned.shape[1] // wide):
        cols = pl.ds(i * wide, wide)
        upd[:, cols] = jnp.dot(direction, turned[:, cols], preferred_element_type=F32)[:OWN].astype(BF16)
        save = pltpu.make_async_copy(upd.at[:, cols], upd_hbm.at[:, cols], sem.at[i])
        save.start()
        saves.append(save)
    for i in range(OWN):
        m_rows[i] = new_first[i : i + 1, :]
        v_rows[i] = new_second[i : i + 1, :]
    saves.append(pltpu.make_async_copy(m_rows, m_hbm, sem.at[4]))
    saves.append(pltpu.make_async_copy(v_rows, v_hbm, sem.at[5]))
    saves[-2].start()
    saves[-1].start()
    for save in saves:
        save.wait()


def on_device(activations, basis, out_grad, first_moment, second_moment):
    d, rank = basis.shape
    tokens, feats = activations.shape
    units = out_grad.shape[1]
    hbm = pl.BlockSpec(memory_space=pltpu.HBM)
    vmem = pl.BlockSpec(memory_space=pltpu.VMEM)
    dma = pltpu.SemaphoreType.DMA
    n_ten, n_xy = len(TENSOR_PEERS), len(XY_PEERS)
    steps = 2 * len(SIZES)
    grad, turned, m, v = pl.pallas_call(
        reduce_kernel,
        out_shape=(
            jax.ShapeDtypeStruct((24, rank), F32),
            jax.ShapeDtypeStruct((rank, d), BF16),
            jax.ShapeDtypeStruct((24, rank), F32),
            jax.ShapeDtypeStruct((24, rank), F32),
        ),
        in_specs=[hbm] * 5,
        out_specs=(vmem,) * 4,
        scratch_shapes=[
            pltpu.VMEM((tokens, feats), BF16),
            pltpu.VMEM((feats, rank), BF16),
            pltpu.VMEM((d, rank), BF16),
            pltpu.VMEM((units, tokens), BF16),
            pltpu.VMEM((OWN, 1, rank), F32),
            pltpu.VMEM((OWN, 1, rank), F32),
            pltpu.VMEM((2, n_ten + 1, TOK, HALF), BF16),
            pltpu.VMEM((2, n_ten, TOK, HALF), BF16),
            pltpu.VMEM((2, n_ten + 1, TOK, HALF), BF16),
            pltpu.VMEM((NX * NY, ALL_ROWS, tokens), BF16),
            pltpu.VMEM((steps, NX * NY, 4 * PAD, HALF), BF16),
            pltpu.VMEM((steps, n_xy, 4 * PAD, HALF), BF16),
            pltpu.VMEM((4 * PAD, HALF), F32),
            pltpu.VMEM((4, 48, HALF), F32),
            pltpu.VMEM((NZ, 48, HALF), BF16),
            pltpu.VMEM((NZ, 48, HALF), BF16),
            dma((12,)),
            dma((2, n_ten)),
            dma((2, n_ten)),
            dma((2, n_ten)),
            dma((2, n_ten)),
            dma((steps, n_xy)),
            dma((steps, n_xy)),
            dma((NZ,)),
            dma((NZ,)),
            pltpu.SemaphoreType.REGULAR((NZ,)),
        ],
        compiler_params=pltpu.CompilerParams(
            collective_id=0, has_side_effects=True, vmem_limit_bytes=40 << 20
        ),
        name="reduce_gradient",
    )(*[
        pltpu.with_memory_space_constraint(a, pltpu.HBM)
        for a in (
            activations,
            basis,
            out_grad.T,
            first_moment.transpose(1, 0, 2),
            second_moment.transpose(1, 0, 2),
        )
    ])
    new_first, new_second, update = pl.pallas_call(
        step_kernel,
        out_shape=(
            jax.ShapeDtypeStruct((OWN, 1, rank), F32),
            jax.ShapeDtypeStruct((OWN, 1, rank), F32),
            jax.ShapeDtypeStruct((OWN, d), BF16),
        ),
        in_specs=[vmem] * 4,
        out_specs=(hbm,) * 3,
        scratch_shapes=[
            pltpu.VMEM((OWN, 1, rank), F32),
            pltpu.VMEM((OWN, 1, rank), F32),
            pltpu.VMEM((OWN, d), BF16),
            dma((6,)),
        ],
        compiler_params=pltpu.CompilerParams(vmem_limit_bytes=16 << 20),
        name="adam_update",
    )(grad, turned, m, v)
    return new_first.transpose(1, 0, 2), new_second.transpose(1, 0, 2), update[None]


def solution(mesh):
    placed = (
        P("dp", "tensor"),
        P(),
        P("dp", "tensor"),
        P("tensor", "dp", None),
        P("tensor", "dp", None),
    )
    return jax.shard_map(
        on_device,
        mesh=mesh,
        in_specs=placed,
        out_specs=(P("tensor", "dp", None), P("tensor", "dp", None), P("tensor", "dp", None)),
        check_vma=False,
    )
```

```python
import functools

import jax
import jax.numpy as jnp
from jax import lax
from jax.experimental import pallas as pl
from jax.experimental.pallas import tpu as pltpu
from jax.sharding import PartitionSpec as P

STEP = 100
MESH = pl.DeviceIdType.MESH
F32 = jnp.float32
BF16 = jnp.bfloat16

NX, NZ, NY = 4, 12, 2
NYH, NC = 4, 2
OWN = 19
PAD = 20
SIZES = (1, 3, 4, 4)
ROWS = (32, 64, 80, 80)
STARTS = (0, 1, 4, 8)
FIRST_ROW = (0, 32, 96, 176)
ALL_ROWS = 256
TOK = 48
HALF = 128

TENSOR_PEERS = ((2, 0), (2, 1), (1, 0), (3, 0), (1, 1), (3, 1), (0, 1))
XY_PEERS = ((2, 1), (2, 0), (1, 1), (3, 1), (1, 0), (3, 0), (0, 1))


def reduce_kernel(
    act_hbm, basis_hbm, og_hbm, m_hbm, v_hbm,
    grad_out, turned_out, m_out, v_out,
    act, rows, basis, og, m_in, v_in,
    part, part_in, code, ogp, chunk, chunk_in, acc, cut, z_out, z_in,
    load_sem, a_send, a_recv, g_send, g_recv, x_send, x_recv, z_send, z_recv, hello,
):
    dp, t = lax.axis_index("dp"), lax.axis_index("tensor")
    x, z, y = dp // (NZ * NY), lax.rem(dp // NY, NZ), lax.rem(dp, NY)
    yh, core = t // NC, lax.rem(t, NC)
    n_ten, n_xy = len(TENSOR_PEERS), len(XY_PEERS)

    def tensor_at(k):
        a, c = TENSOR_PEERS[k]
        return lax.rem(yh + a, NYH) * NC + lax.rem(core + c, NC)

    def xy_at(place):
        dx, dy = place
        return lax.rem(x + dx, NX), lax.rem(y + dy, NY)

    def dp_at(px, pz, py):
        return (lax.rem(px, NX) * NZ + lax.rem(pz, NZ)) * NY + lax.rem(py, NY)

    barrier = pltpu.get_barrier_semaphore()

    def signal(to_dp, to_t):
        pl.semaphore_signal(barrier, inc=1, device_id=(to_dp, to_t), device_id_type=MESH)

    for k in range(n_ten):
        signal(dp, tensor_at(k))
    for dx, dy in XY_PEERS:
        signal(dp_at(x + dx, z, y + dy), t)
    for to in range(NZ - 1, 0, -1):

        @pl.when(z < to)
        def _():
            signal(dp_at(x, to, y), t)

    tokens, feats = act.shape
    start = pl.multiple_of(t * feats, feats)
    n_cut = 4
    first_loads = []
    for i in range(n_cut):
        n = feats // n_cut
        first_loads.append(
            pltpu.make_async_copy(
                basis_hbm.at[pl.ds(start + i * n, n)], rows.at[pl.ds(i * n, n)], load_sem.at[i]
            )
        )
        n = tokens // n_cut
        first_loads.append(
            pltpu.make_async_copy(
                act_hbm.at[pl.ds(i * n, n)], act.at[pl.ds(i * n, n)], load_sem.at[n_cut + i]
            )
        )
    og_load = pltpu.make_async_copy(og_hbm, og, load_sem.at[2 * n_cut])
    m_load = pltpu.make_async_copy(m_hbm, m_in, load_sem.at[2 * n_cut + 1])
    v_load = pltpu.make_async_copy(v_hbm, v_in, load_sem.at[2 * n_cut + 2])
    basis_load = pltpu.make_async_copy(basis_hbm, basis, load_sem.at[2 * n_cut + 3])
    for load in first_loads:
        load.start()

    for load in first_loads:
        load.wait()
    og_load.start()
    m_load.start()
    v_load.start()
    basis_load.start()
    a_copies = []
    for h in range(2):
        coded = jnp.dot(act[...], rows[:, h * HALF : (h + 1) * HALF], preferred_element_type=F32)
        part[h] = coded.astype(BF16).reshape(part.shape[1:])
        if h == 0:
            pl.semaphore_wait(barrier, n_ten + n_xy + z)
        for k in range(n_ten):
            peer = tensor_at(k)
            copy = pltpu.make_async_remote_copy(
                src_ref=part.at[h, peer], dst_ref=part_in.at[h, k],
                send_sem=a_send.at[h, k], recv_sem=a_recv.at[h, k],
                device_id=(dp, peer), device_id_type=MESH,
            )
            copy.start()
            a_copies.append(copy)

    for to in range(NZ - 1):

        @pl.when(z > to)
        def _():
            pl.semaphore_signal(hello.at[z], inc=1, device_id=(dp_at(x, to, y), t), device_id_type=MESH)

    og_load.wait()
    n_in = NZ * NY * OWN
    window = n_in + 8
    r = lax.broadcasted_iota(jnp.int32, (NY * ALL_ROWS, 1), 0)
    to_y, row = r // ALL_ROWS, lax.rem(r, ALL_ROWS)
    source = jnp.full_like(r, -window)
    for g in range(len(SIZES)):
        for i in range(SIZES[g]):
            at = FIRST_ROW[g] + i * PAD
            inside = (row >= at) & (row < at + OWN)
            source = jnp.where(inside, ((STARTS[g] + i) * NY + to_y) * OWN + row - at, source)
    c = lax.broadcasted_iota(jnp.int32, (NY * ALL_ROWS, window), 1)
    picks = [jnp.where(c == source + shift, 1.0, 0.0).astype(BF16) for shift in (0, 8)]
    for ox in range(NX):
        shift = ox * n_in % 16
        first = ox * n_in - shift
        moved = jnp.dot(picks[shift // 8], og[first : first + window, :], preferred_element_type=F32)
        ogp[ox * NY : (ox + 1) * NY] = moved.astype(BF16).reshape(NY, ALL_ROWS, moved.shape[1])
    cut[...] = jnp.zeros_like(cut)

    g_copies = []
    for h in range(2):
        total = part[h, t].astype(F32)
        for k in range(n_ten):
            a_copies[h * n_ten + k].wait_recv()
            total = total + part_in[h, k].astype(F32)
        code[h, t] = total.astype(BF16)
        for k in range(n_ten):
            copy = pltpu.make_async_remote_copy(
                src_ref=code.at[h, t], dst_ref=code.at[h, t],
                send_sem=g_send.at[h, k], recv_sem=g_recv.at[h, k],
                device_id=(dp, tensor_at(k)), device_id_type=MESH,
            )
            copy.start()
            g_copies.append(copy)

    m_load.wait()
    v_load.wait()
    m_out[...] = jnp.zeros_like(m_out)
    v_out[...] = jnp.ones_like(v_out)
    for i in range(OWN):
        m_out[i : i + 1, :] = m_in[i]
        v_out[i : i + 1, :] = v_in[i]
    basis_load.wait()
    wide = 1024
    for i in range(basis.shape[0] // wide):
        turned_out[:, i * wide : (i + 1) * wide] = basis[i * wide : (i + 1) * wide, :].T

    def z_copy(to):
        return pltpu.make_async_remote_copy(
            src_ref=z_out.at[to], dst_ref=z_in.at[z], send_sem=z_send.at[to], recv_sem=z_recv.at[z],
            device_id=(dp_at(x, to, y), t), device_id_type=MESH,
        )

    x_copies = {}

    def share(h, g):
        coded = code[h].reshape((n_ten + 1) * TOK, HALF)
        at, n = h * len(SIZES) + g, ROWS[g]
        rows_of = ogp[:, FIRST_ROW[g] : FIRST_ROW[g] + n, :].reshape(NX * NY * n, ogp.shape[2])
        term = jnp.dot(rows_of, coded, preferred_element_type=F32)
        chunk[at, :, 0:n, :] = term.astype(BF16).reshape(NX * NY, n, HALF)
        x_copies[at] = []
        for k in range(n_xy):
            px, py = xy_at(XY_PEERS[k])
            copy = pltpu.make_async_remote_copy(
                src_ref=chunk.at[at, px * NY + py, pl.ds(0, n)], dst_ref=chunk_in.at[at, k, pl.ds(0, n)],
                send_sem=x_send.at[at, k], recv_sem=x_recv.at[at, k],
                device_id=((px * NZ + z) * NY + py, t), device_id_type=MESH,
            )
            copy.start()
            x_copies[at].append(copy)

    def collect(g):
        n = ROWS[g]
        for h in range(2):
            at = h * len(SIZES) + g
            total = chunk[at, x * NY + y, 0:n, :].astype(F32)
            for k in range(n_xy):
                x_copies[at][k].wait_recv()
                total = total + chunk_in[at, k, 0:n, :].astype(F32)
            acc[0:n, :] = total
            for i in range(SIZES[g]):
                cut[i, 24 * h : 24 * h + PAD, :] = acc[i * PAD : (i + 1) * PAD, :]
        for i in range(SIZES[g]):
            to = STARTS[g] + i
            z_out[to] = cut[i].astype(BF16)

            @pl.when(z < to)
            def _():
                pl.semaphore_wait(hello.at[to], 1)

            @pl.when(z != to)
            def _():
                z_copy(to).start()

    for h in range(2):
        for k in range(n_ten):
            g_copies[h * n_ten + k].wait_recv()
        share(h, 0)
    for g in range(len(SIZES)):
        if g + 1 < len(SIZES):
            for h in range(2):
                share(h, g + 1)
        collect(g)
    total = z_out[z].astype(F32)
    for ahead in range(1, NZ):
        sender = lax.rem(z + ahead, NZ)
        pltpu.make_async_copy(z_in.at[sender], z_in.at[sender], z_recv.at[sender]).wait()
        total = total + z_in[sender].astype(F32)
    grad_out[...] = jnp.concatenate([total[0:24], total[24:48]], axis=1)
    for to in range(NZ):

        @pl.when(z != to)
        def _():
            z_copy(to).wait_send()

    for copy in a_copies + g_copies + sum(x_copies.values(), []):
        copy.wait_send()


def step_kernel(grad, turned, m, v, m_hbm, v_hbm, upd_hbm, m_rows, v_rows, upd, sem):
    g = grad[...]
    new_first = 0.9 * m[...] + 0.1 * g
    new_second = 0.999 * v[...] + 0.001 * g * g
    first_hat = new_first / (1.0 - 0.9**STEP)
    second_hat = new_second / (1.0 - 0.999**STEP)
    direction = first_hat / (jnp.sqrt(second_hat) + 1e-08)
    direction = jnp.concatenate([direction, jnp.zeros((8, direction.shape[1]), F32)], axis=0).astype(BF16)
    wide = 2048
    saves = []
    for i in range(turned.shape[1] // wide):
        cols = pl.ds(i * wide, wide)
        upd[:, cols] = jnp.dot(direction, turned[:, cols], preferred_element_type=F32)[:OWN].astype(BF16)
        save = pltpu.make_async_copy(upd.at[:, cols], upd_hbm.at[:, cols], sem.at[i])
        save.start()
        saves.append(save)
    for i in range(OWN):
        m_rows[i] = new_first[i : i + 1, :]
        v_rows[i] = new_second[i : i + 1, :]
    saves.append(pltpu.make_async_copy(m_rows, m_hbm, sem.at[4]))
    saves.append(pltpu.make_async_copy(v_rows, v_hbm, sem.at[5]))
    saves[-2].start()
    saves[-1].start()
    for save in saves:
        save.wait()


def on_device(activations, basis, out_grad, first_moment, second_moment):
    d, rank = basis.shape
    tokens, feats = activations.shape
    units = out_grad.shape[1]
    hbm = pl.BlockSpec(memory_space=pltpu.HBM)
    vmem = pl.BlockSpec(memory_space=pltpu.VMEM)
    dma = pltpu.SemaphoreType.DMA
    n_ten, n_xy = len(TENSOR_PEERS), len(XY_PEERS)
    steps = 2 * len(SIZES)
    grad, turned, m, v = pl.pallas_call(
        reduce_kernel,
        out_shape=(
            jax.ShapeDtypeStruct((24, rank), F32),
            jax.ShapeDtypeStruct((rank, d), BF16),
            jax.ShapeDtypeStruct((24, rank), F32),
            jax.ShapeDtypeStruct((24, rank), F32),
        ),
        in_specs=[hbm] * 5,
        out_specs=(vmem,) * 4,
        scratch_shapes=[
            pltpu.VMEM((tokens, feats), BF16),
            pltpu.VMEM((feats, rank), BF16),
            pltpu.VMEM((d, rank), BF16),
            pltpu.VMEM((units, tokens), BF16),
            pltpu.VMEM((OWN, 1, rank), F32),
            pltpu.VMEM((OWN, 1, rank), F32),
            pltpu.VMEM((2, n_ten + 1, TOK, HALF), BF16),
            pltpu.VMEM((2, n_ten, TOK, HALF), BF16),
            pltpu.VMEM((2, n_ten + 1, TOK, HALF), BF16),
            pltpu.VMEM((NX * NY, ALL_ROWS, tokens), BF16),
            pltpu.VMEM((steps, NX * NY, 4 * PAD, HALF), BF16),
            pltpu.VMEM((steps, n_xy, 4 * PAD, HALF), BF16),
            pltpu.VMEM((4 * PAD, HALF), F32),
            pltpu.VMEM((4, 48, HALF), F32),
            pltpu.VMEM((NZ, 48, HALF), BF16),
            pltpu.VMEM((NZ, 48, HALF), BF16),
            dma((12,)),
            dma((2, n_ten)),
            dma((2, n_ten)),
            dma((2, n_ten)),
            dma((2, n_ten)),
            dma((steps, n_xy)),
            dma((steps, n_xy)),
            dma((NZ,)),
            dma((NZ,)),
            pltpu.SemaphoreType.REGULAR((NZ,)),
        ],
        compiler_params=pltpu.CompilerParams(
            collective_id=0, has_side_effects=True, vmem_limit_bytes=40 << 20
        ),
        name="reduce_gradient",
    )(*[
        pltpu.with_memory_space_constraint(a, pltpu.HBM)
        for a in (
            activations,
            basis,
            out_grad.T,
            first_moment.transpose(1, 0, 2),
            second_moment.transpose(1, 0, 2),
        )
    ])
    new_first, new_second, update = pl.pallas_call(
        step_kernel,
        out_shape=(
            jax.ShapeDtypeStruct((OWN, 1, rank), F32),
            jax.ShapeDtypeStruct((OWN, 1, rank), F32),
            jax.ShapeDtypeStruct((OWN, d), BF16),
        ),
        in_specs=[vmem] * 4,
        out_specs=(hbm,) * 3,
        scratch_shapes=[
            pltpu.VMEM((OWN, 1, rank), F32),
            pltpu.VMEM((OWN, 1, rank), F32),
            pltpu.VMEM((OWN, d), BF16),
            dma((6,)),
        ],
        compiler_params=pltpu.CompilerParams(vmem_limit_bytes=16 << 20),
        name="adam_update",
    )(grad, turned, m, v)
    return new_first.transpose(1, 0, 2), new_second.transpose(1, 0, 2), update[None]


def solution(mesh):
    placed = (
        P("dp", "tensor"),
        P(),
        P("dp", "tensor"),
        P("tensor", "dp", None),
        P("tensor", "dp", None),
    )
    return jax.shard_map(
        on_device,
        mesh=mesh,
        in_specs=placed,
        out_specs=(P("tensor", "dp", None), P("tensor", "dp", None), P("tensor", "dp", None)),
        check_vma=False,
    )
```
